128 devices in a mesh: ctx: 16 (over y, x_hi, core), tp: 8 (over z, x_lo).
Axes of the slice: x: 4 (x_hi: 2, x_lo: 2; x = x_hi * 2 + x_lo), y: 4, z: 4, core: 2. Of those that a mesh axis runs over, the one named last changes fastest.
Arguments:
- query_rows: bfloat16 [4096, 8192], P('ctx', 'tp'), may hold values from -210 to 210
- key_rows: bfloat16 [4096, 1024], P('ctx', 'tp'), may hold values from -20 to 20
- value_rows: bfloat16 [4096, 1024], P('ctx', 'tp'), may hold values from -6 to 6
- grad_out: bfloat16 [4096, 8192], P('ctx', 'tp'), may hold values from -12 to 12
- doc_ids: int32 [32], replicated, may hold values from 0 to 3, never falling along the last dimension, each value on 1 to 16 neighbouring positions
- w_query: bfloat16 [8192, 8192], P(None, 'tp'), may hold values from -0.47851562 to 0.47851562
- w_key: bfloat16 [8192, 1024], P(None, 'tp'), may hold values from -0.47851562 to 0.47851562
- w_value: bfloat16 [8192, 1024], P(None, 'tp'), may hold values from -0.47851562 to 0.47851562
Outputs:
- d_input: bfloat16 [4096, 8192], P(('ctx', 'tp'))
The draws below stay inside these ranges and needn't reach their ends.
Inputs may be any that keep to these rules, and one draw needn't show every extreme that they name: `doc_ids`: ids never fall from block to block; each of the 4 documents covers 1 to 16 blocks, and one of them covers exactly 16 blocks.
All inputs are finite; a program needn't handle non-finite values.
Results may differ from the reference program's by a relative error of at most 0.024.
Values may be sent and summed in bfloat16 or wider, within the bound.
A program may use at most 128 MiB of HBM per device.

```python
import math
import jax
import jax.numpy as jnp
import numpy as np
from jax import lax

D = 8192
HEADS = 64
KV_HEADS = 8
HEAD_DIM = 128
BLK = 128
TOKENS = 4096
BLOCKS = 32
DOCS = 4
N_TP = 8


def drawn_rows():
    places = jnp.arange(TOKENS, dtype=jnp.int32)
    return (places % BLK == BLK // 2) & (places // BLK % 3 == 0)


def shared_keys(key, spread):
    base = jnp.clip(jax.random.normal(jax.random.fold_in(key, 101), (TOKENS, KV_HEADS * HEAD_DIM), jnp.float32), -6.0, 6.0)
    uniform_draw = jax.random.uniform(jax.random.fold_in(key, 102), (TOKENS, 1), jnp.float32)
    planted = drawn_rows()
    before_one = jnp.roll(planted, -1)
    before_two = jnp.roll(planted, -2)
    near_rows = (before_one | before_two)[:, None]
    row_scale = jnp.where(near_rows, 1.0, jnp.exp(spread * (2.0 * uniform_draw - 1.0)))
    scaled = base * row_scale
    return jnp.where(before_two[:, None], scaled, scaled)


def draw_key_rows(key, part):
    spread = 0.0
    return shared_keys(key, spread).astype(jnp.bfloat16)


def draw_query_rows(key, part):
    key = jax.random.fold_in(key, 7)
    base = jnp.clip(jax.random.normal(jax.random.fold_in(key, 1), (TOKENS, HEADS * HEAD_DIM), jnp.float32), -6.0, 6.0)
    planted = drawn_rows()[:, None]
    return jnp.where(planted, base, base).astype(jnp.bfloat16)


def block_levels(rng, dims, cuts, low, largest):
    factor_of, own = 1.0, jax.random.fold_in(rng, 6)
    for dim, shards_of in cuts:
        heights = jnp.exp(jax.random.uniform(jax.random.fold_in(own, dim), (shards_of,), jnp.float32, low / len(cuts), largest / len(cuts)))
        factor_of = factor_of * jnp.repeat(heights, dims[dim] // shards_of).reshape([-1 if axis == dim else 1 for axis in range(len(dims))])
    return factor_of


def split_up(number_of, total, limit, skew):
    loads = [(1 << 20) // math.isqrt(standing ** skew) + 1 for standing in range(2, number_of + 1)]
    spare, given = total - limit - (number_of - 1), [1] * (number_of - 1)
    while spare > 0:
        candidates = [i for i in range(number_of - 1) if given[i] < limit]
        pool, left = sum([loads[i] for i in candidates]), spare
        for i in candidates:
            extra = min(limit - given[i], max(1, left * loads[i] // pool), spare)
            given[i] = given[i] + extra
            spare = spare - extra
    return np.array([limit] + given)


def uneven_parts(rng, number_of, total, limit, skew):
    if number_of == 2:
        one = jax.random.randint(rng, (), max(1, total - limit), min(limit, total - 1) + 1)
        return jnp.stack([one, total - one])
    lengths = jnp.asarray(split_up(number_of, total, limit, skew), jnp.int32)
    pairs = (number_of - 1) // 2
    giver, taker = lengths[1:1 + 2 * pairs:2], lengths[2:2 + 2 * pairs:2]
    slack = jnp.minimum(giver - 1, limit - taker)
    moved = jax.random.randint(jax.random.fold_in(rng, 1), (pairs,), 0, 1 << 20) % (slack + 1)
    lengths = lengths.at[1:1 + 2 * pairs:2].set(giver - moved).at[2:2 + 2 * pairs:2].set(taker + moved)
    return lengths[jax.random.permutation(jax.random.fold_in(rng, 2), number_of)]


def centred(key, shape, scale, bound, pieces=(), held_as=jnp.bfloat16):
    entries = jax.random.normal(key, shape, jnp.float32) * scale
    if len(pieces) > 0:
        entries = block_levels(key, shape, pieces, -0.22, 0.18) * entries
    return jnp.clip(entries, min=-bound, max=bound).astype(held_as)


def setup_inputs(seed: int = 0) -> dict:
    key_of = jax.random.split(jax.random.key(seed), 9)
    return {
        "query_rows": draw_query_rows(jax.random.fold_in(key_of[8], 71), 0),
        "key_rows": draw_key_rows(jax.random.fold_in(key_of[8], 71), 0),
        "value_rows": centred(key_of[2], (TOKENS, KV_HEADS * HEAD_DIM), 1.0, 6.0, ((0, 16), (1, 8))),
        "grad_out": centred(key_of[3], (TOKENS, HEADS * HEAD_DIM), 2.0, 12.0, ((0, 16), (1, 8))),
        "doc_ids": jnp.searchsorted(jnp.cumsum(uneven_parts(key_of[4], DOCS, BLOCKS, BLOCKS // 2, 1)), jnp.arange(BLOCKS), side="right").astype(jnp.int32),
        "w_query": centred(key_of[5], (D, HEADS * HEAD_DIM), 0.08, 0.47851562, ((1, 8),)),
        "w_key": centred(key_of[6], (D, KV_HEADS * HEAD_DIM), 0.08, 0.47851562, ((1, 8),)),
        "w_value": centred(key_of[7], (D, KV_HEADS * HEAD_DIM), 0.08, 0.47851562, ((1, 8),)),
    }


THETA = 500000.0
NEGATIVE = -1e30


def rope_back(gradient, first_pos):
    tok_rows = gradient.shape[0]
    head_width = gradient.shape[-1]
    half_width = head_width // 2
    places = (first_pos + jnp.arange(tok_rows, dtype=jnp.int32)).astype(jnp.float32)
    frequencies = jnp.exp(jnp.arange(half_width, dtype=jnp.float32) * (-2.0 * math.log(THETA) / head_width))
    angles = places[:, None] * frequencies[None, :]
    cosine = jnp.cos(angles)[:, None, :]
    sine_part = jnp.sin(angles)[:, None, :]
    first_half = gradient[..., :half_width]
    second_half = gradient[..., half_width:]
    return jnp.concatenate([first_half * cosine + second_half * sine_part, second_half * cosine - first_half * sine_part], axis=-1)


def reference(query_rows, key_rows, value_rows, grad_out, doc_ids, w_query, w_key, w_value):
    group_size = HEADS // KV_HEADS
    score_scale = HEAD_DIM ** -0.5
    places = jnp.arange(TOKENS, dtype=jnp.int32)
    token_docs = jnp.repeat(doc_ids, BLK)
    allowed = (places[None, :] <= places[:, None]) & (token_docs[None, :] == token_docs[:, None])

    def head_grads(head_index):
        kv_index = head_index // group_size
        query_head = lax.dynamic_slice_in_dim(query_rows, head_index * HEAD_DIM, HEAD_DIM, 1)
        grad_head = lax.dynamic_slice_in_dim(grad_out, head_index * HEAD_DIM, HEAD_DIM, 1)
        key_head = lax.dynamic_slice_in_dim(key_rows, kv_index * HEAD_DIM, HEAD_DIM, 1)
        value_head = lax.dynamic_slice_in_dim(value_rows, kv_index * HEAD_DIM, HEAD_DIM, 1)
        scores = jnp.dot(query_head, key_head.T, preferred_element_type=jnp.float32) * score_scale
        grad_probs = jnp.dot(grad_head, value_head.T, preferred_element_type=jnp.float32)
        row_top = jnp.max(jnp.where(allowed, scores, NEGATIVE), axis=1, keepdims=True)
        weights = jnp.where(allowed, jnp.exp(scores - row_top), 0.0)
        exp_total = jnp.sum(weights, axis=1, keepdims=True)
        log_total = row_top + jnp.log(exp_total)
        average = jnp.sum(weights * grad_probs, axis=1, keepdims=True) / exp_total
        probabilities = jnp.where(allowed, jnp.exp(scores - log_total), 0.0)
        dscores = (probabilities * (grad_probs - average)).astype(jnp.bfloat16)
        probs_low = probabilities.astype(jnp.bfloat16)
        query_grad = jnp.dot(dscores, key_head, preferred_element_type=jnp.float32) * score_scale
        key_grad = jnp.dot(dscores.T, query_head, preferred_element_type=jnp.float32) * score_scale
        value_grad = jnp.dot(probs_low.T, grad_head, preferred_element_type=jnp.float32)
        return query_grad, key_grad, value_grad

    query_all, key_all, value_all = lax.map(head_grads, jnp.arange(HEADS, dtype=jnp.int32))
    query_grad = jnp.transpose(query_all, (1, 0, 2))
    key_grad = jnp.transpose(jnp.sum(key_all.reshape(KV_HEADS, group_size, TOKENS, HEAD_DIM), axis=1), (1, 0, 2))
    value_grad = jnp.transpose(jnp.sum(value_all.reshape(KV_HEADS, group_size, TOKENS, HEAD_DIM), axis=1), (1, 0, 2))
    query_in = rope_back(query_grad, 0).reshape(TOKENS, HEADS * HEAD_DIM).astype(jnp.bfloat16)
    key_in = rope_back(key_grad, 0).reshape(TOKENS, KV_HEADS * HEAD_DIM).astype(jnp.bfloat16)
    value_in = value_grad.reshape(TOKENS, KV_HEADS * HEAD_DIM).astype(jnp.bfloat16)
    query_cols = (HEADS // N_TP) * HEAD_DIM
    key_cols = (KV_HEADS // N_TP) * HEAD_DIM
    summed = jnp.zeros((TOKENS, D), jnp.float32)
    for member in range(N_TP):
        q_low = member * query_cols
        k_low = member * key_cols
        term_part = jnp.dot(query_in[:, q_low:q_low + query_cols], w_query[:, q_low:q_low + query_cols].T, preferred_element_type=jnp.float32)
        term_part = term_part + jnp.dot(key_in[:, k_low:k_low + key_cols], w_key[:, k_low:k_low + key_cols].T, preferred_element_type=jnp.float32)
        term_part = term_part + jnp.dot(value_in[:, k_low:k_low + key_cols], w_value[:, k_low:k_low + key_cols].T, preferred_element_type=jnp.float32)
        rounded = lax.optimization_barrier(term_part.astype(jnp.bfloat16))
        summed = summed + rounded.astype(jnp.float32)
    return summed.astype(jnp.bfloat16)
```

```python
import functools
import math

import jax
import jax.numpy as jnp
from jax import lax
from jax.experimental import pallas as pl
from jax.experimental.pallas import tpu as pltpu
from jax.sharding import PartitionSpec as P

HEADS = 64
KV_HEADS = 8
HEAD_DIM = 128
BLK = 128
GROUP = HEADS // KV_HEADS
BLOCKS = 32
THETA = 500000.0
NEGATIVE = -1e30
ROWS = 256
FAR = 4
SCALE = HEAD_DIM ** (-0.5)
LOG2_SCALE = SCALE * math.log2(math.e)
STEPS = 8
WIDTH = 1024
WIDE_X = 640
WIDE_Z = WIDTH - WIDE_X
DEPTH = GROUP * HEAD_DIM + 2 * HEAD_DIM
F32 = jnp.float32
BF16 = jnp.bfloat16


def dot_nt(left, right):
    return lax.dot_general(left, right, (((1,), (1,)), ((), ())), preferred_element_type=F32)


def dot_nn(left, right):
    return lax.dot_general(left, right, (((1,), (0,)), ((), ())), preferred_element_type=F32)


def remote(src, dst, send, recv, **device):
    return pltpu.make_async_remote_copy(
        src_ref=src, dst_ref=dst, send_sem=send, recv_sem=recv,
        device_id=device, device_id_type=pl.DeviceIdType.MESH,
    )


def attention_kernel(
    q_hbm, k_hbm, v_hbm, g_hbm, docs, a_ref,
    kv, qs, gs, ws, gps, tops, top, total, weighted, dqt, kt, acc, stage, pair, back, cosine, sine,
    q_sem, g_sem, own_sem, kv_send, kv_recv, pass_send, pair_send, pair_recv, back_send, back_recv,
):
    c = lax.axis_index("ctx")
    size = lax.axis_size("ctx")
    chips = size // 2
    chip, core = c // 2, c % 2
    sibling = c + 1 - 2 * core

    q_loads = [pltpu.make_async_copy(q_hbm.at[:, pl.ds(h * HEAD_DIM, HEAD_DIM)], qs.at[h], q_sem.at[h]) for h in range(GROUP)]
    g_loads = [pltpu.make_async_copy(g_hbm.at[:, pl.ds(h * HEAD_DIM, HEAD_DIM)], gs.at[h], g_sem.at[h]) for h in range(GROUP)]
    own_loads = [pltpu.make_async_copy(k_hbm, kv.at[0, 0], own_sem.at[0]), pltpu.make_async_copy(v_hbm, kv.at[0, 1], own_sem.at[1])]
    for load in own_loads + q_loads + g_loads:
        load.start()

    barrier = pltpu.get_barrier_semaphore()
    pl.semaphore_signal(barrier, inc=1, device_id={"ctx": sibling}, device_id_type=pl.DeviceIdType.MESH)
    for m in range(1, chips):
        pl.semaphore_signal(barrier, inc=1, device_id={"ctx": (c + 2 * m) % size}, device_id_type=pl.DeviceIdType.MESH)
    pl.semaphore_wait(barrier, chips)

    for load in own_loads:
        load.wait()

    def key_copy(m):
        return remote(kv.at[0], kv.at[2 * m], kv_send.at[m], kv_recv.at[2 * m], ctx=(c + 2 * m) % size)

    def pass_copy(m):
        slot = 2 * m + 1 - 2 * core
        return remote(kv.at[2 * m], kv.at[slot], pass_send.at[m], kv_recv.at[slot], ctx=sibling)

    def passes(m):
        return (chip >= m) & ((m > 0) | (core == 0)) & ((m < FAR) | (core == 1))

    @pl.when(core == 0)
    def _():
        pass_copy(0).start()

    for m in range(1, FAR + 1):
        @pl.when(chip + m < chips)
        def _():
            key_copy(m).start()

    places = (c * ROWS + lax.broadcasted_iota(jnp.int32, (ROWS, HEAD_DIM), 0)).astype(F32)
    lanes = lax.broadcasted_iota(jnp.int32, (ROWS, HEAD_DIM), 1)
    half = HEAD_DIM // 2
    pair_lane = jnp.where(lanes < half, lanes, lanes - half).astype(F32)
    angles = places * jnp.exp(pair_lane * (-2.0 * math.log(THETA) / HEAD_DIM))
    cosine[...] = jnp.cos(angles)
    sine[...] = jnp.where(lanes < half, 1.0, -1.0) * jnp.sin(angles)

    def rope_back(y):
        return y * cosine[...] + pltpu.roll(y, half, 1) * sine[...]

    starts = []
    for block in range(2):
        document = docs[2 * c + block]
        starts.append(sum([(docs[b] < document).astype(jnp.int32) for b in range(BLOCKS)]))
    lane = lax.broadcasted_iota(jnp.int32, (1, ROWS), 1)
    start_row = jnp.where(lane < BLK, starts[0], starts[1])

    dqt[...] = jnp.zeros_like(dqt)
    for load in q_loads + g_loads:
        load.wait()

    def tile_stats(d, first):
        key_block = 2 * (c - d)
        bias = [jnp.where(key_block + b >= start_row, 0.0, NEGATIVE) for b in range(2)]

        def head(h, carry):
            s = dot_nt(kv[d, 0], qs[h]) * LOG2_SCALE
            gp = dot_nt(kv[d, 1], gs[h])
            s = jnp.concatenate([s[:BLK] + bias[0], s[BLK:] + bias[1]], axis=0)
            if first:
                key_at = lax.broadcasted_iota(jnp.int32, (ROWS, ROWS), 0)
                query_at = lax.broadcasted_iota(jnp.int32, (ROWS, ROWS), 1)
                s = jnp.where(key_at <= query_at, s, NEGATIVE)
            here = jnp.max(s, axis=0, keepdims=True)
            if first:
                new = here
            else:
                old = top[h]
                new = jnp.maximum(old, here)
            w = jnp.exp2(s - new)
            part = jnp.sum(w, axis=0, keepdims=True)
            part_weighted = jnp.sum(w * gp, axis=0, keepdims=True)
            if first:
                total[h] = part
                weighted[h] = part_weighted
            else:
                factor = jnp.exp2(old - new)
                total[h] = total[h] * factor + part
                weighted[h] = weighted[h] * factor + part_weighted
            top[h] = new
            tops[d, h] = new
            ws[d, h] = w.astype(BF16)
            gps[d, h] = gp.astype(BF16)
            return carry

        lax.fori_loop(0, GROUP, head, 0)

    far = 2 * FAR

    def far_stats():
        bias = jnp.where(2 * (c - far) + 1 >= starts[0], 0.0, NEGATIVE)

        def head(h, carry):
            s = dot_nt(kv[far, 0, BLK:], qs[h, :BLK]) * LOG2_SCALE + bias
            gp = dot_nt(kv[far, 1, BLK:], gs[h, :BLK])
            old = top[h, :, :BLK]
            new = jnp.maximum(old, jnp.max(s, axis=0, keepdims=True))
            w = jnp.exp2(s - new)
            factor = jnp.exp2(old - new)
            total[h, :, :BLK] = total[h, :, :BLK] * factor + jnp.sum(w, axis=0, keepdims=True)
            weighted[h, :, :BLK] = weighted[h, :, :BLK] * factor + jnp.sum(w * gp, axis=0, keepdims=True)
            top[h, :, :BLK] = new
            tops[far, h, :, :BLK] = new
            ws[far, h, :BLK, :BLK] = w.astype(BF16)
            gps[far, h, :BLK, :BLK] = gp.astype(BF16)
            return carry

        lax.fori_loop(0, GROUP, head, 0)

    tile_stats(0, True)

    def near(d, carry):
        m = (d + 1) // 2

        @pl.when((d % 2 == 1) & (chip >= m))
        def _():
            key_copy(m).wait_recv()

            @pl.when(passes(m))
            def _():
                pass_copy(m).start()

        @pl.when(c >= d)
        def _():
            @pl.when(d % 2 == 1)
            def _():
                remote(kv.at[d], kv.at[d], pass_send.at[0], kv_recv.at[d], ctx=sibling).wait_recv()

            tile_stats(d, False)

        return carry

    lax.fori_loop(1, far, near, 0)

    @pl.when(c >= far)
    def _():
        far_stats()

    def finish(h, carry):
        inverse = 1.0 / total[h]
        total[h] = inverse
        weighted[h] = weighted[h] * inverse
        return carry

    lax.fori_loop(0, GROUP, finish, 0)

    def tile_grads(d):
        kt[...] = jnp.transpose(kv[d, 0].astype(F32)).astype(BF16)
        acc[...] = jnp.zeros_like(acc)

        def head(h, carry):
            p = ws[d, h].astype(F32) * (jnp.exp2(tops[d, h] - top[h]) * total[h])
            ds = (p * (gps[d, h].astype(F32) - weighted[h])).astype(BF16)
            acc[0] += dot_nn(ds, qs[h])
            acc[1] += dot_nn(p.astype(BF16), gs[h])
            dqt[h] += dot_nn(kt[...], ds)
            return carry

        lax.fori_loop(0, GROUP, head, 0)

    def far_grads():
        kt[...] = jnp.transpose(kv[far, 0].astype(F32)).astype(BF16)
        acc[...] = jnp.zeros_like(acc)

        def head(h, carry):
            p = ws[far, h, :BLK, :BLK].astype(F32) * (jnp.exp2(tops[far, h, :, :BLK] - top[h, :, :BLK]) * total[h, :, :BLK])
            ds = (p * (gps[far, h, :BLK, :BLK].astype(F32) - weighted[h, :, :BLK])).astype(BF16)
            acc[0, BLK:] += dot_nn(ds, qs[h, :BLK])
            acc[1, BLK:] += dot_nn(p.astype(BF16), gs[h, :BLK])
            dqt[h, :, :BLK] += dot_nn(kt[:, BLK:], ds)
            return carry

        lax.fori_loop(0, GROUP, head, 0)

    def pair_copy(d):
        slot = (d + 1 - 2 * core) // 2
        return remote(stage.at[d], pair.at[slot], pair_send.at[d // 2], pair_recv.at[slot], ctx=sibling)

    def pair_wait(m):
        remote(stage.at[0], pair.at[m], pair_send.at[0], pair_recv.at[m], ctx=sibling).wait_recv()

    def back_copy(m):
        return remote(stage.at[2 * m], back.at[m], back_send.at[m], back_recv.at[m], ctx=(c + size - 2 * m) % size)

    def odd(d):
        @pl.when(c >= d)
        def _():
            tile_grads(d)
            stage[d] = acc[...].astype(BF16)
            pair_copy(d).start()

    def even(m, grads):
        @pl.when(chip >= m)
        def _():
            grads()

            @pl.when((m < FAR) | (core == 1))
            def _():
                pair_wait(m)
                acc[...] += pair[m].astype(F32)

            stage[2 * m] = acc[...].astype(BF16)
            back_copy(m).start()

    odd(far - 1)
    even(FAR, far_grads)

    def inward(step, carry):
        m = FAR - 1 - step
        odd(2 * m - 1)
        even(m, lambda: tile_grads(2 * m))
        return carry

    lax.fori_loop(0, FAR - 1, inward, 0)
    tile_grads(0)

    def place(value, columns):
        for t in range(8):
            to = (t % 2) * 4 + t // 2
            a_ref[to * 32:(to + 1) * 32, columns] = value[t * 32:(t + 1) * 32]

    for h in range(GROUP):
        y = jnp.transpose(dqt[h]) * SCALE
        place(rope_back(y).astype(BF16), slice(h * HEAD_DIM, (h + 1) * HEAD_DIM))

    @pl.when(core == 0)
    def _():
        pair_wait(0)
        acc[...] += pair[0].astype(F32)

    for m in range(FAR, 0, -1):
        @pl.when(chip + m < chips)
        def _():
            back_copy(m).wait_recv()
            acc[...] += back[m].astype(F32)

    base = GROUP * HEAD_DIM
    place(rope_back(acc[0] * SCALE).astype(BF16), slice(base, base + HEAD_DIM))
    place(acc[1].astype(BF16), slice(base + HEAD_DIM, base + 2 * HEAD_DIM))

    for m in range(FAR + 1):
        @pl.when(passes(m))
        def _():
            pass_copy(m).wait_send()

    for m in range(1, FAR + 1):
        @pl.when(chip + m < chips)
        def _():
            key_copy(m).wait_send()

        @pl.when(c >= 2 * m - 1)
        def _():
            pair_copy(2 * m - 1).wait_send()

        @pl.when(chip >= m)
        def _():
            back_copy(m).wait_send()


def attention(q, k, v, g, docs):
    any_spec = pl.BlockSpec(memory_space=pl.ANY)
    slots = 2 * FAR + 1
    dma = pltpu.SemaphoreType.DMA
    return pl.pallas_call(
        attention_kernel,
        out_shape=jax.ShapeDtypeStruct((ROWS, DEPTH), BF16),
        in_specs=[any_spec] * 4 + [pl.BlockSpec(memory_space=pltpu.SMEM)],
        out_specs=pl.BlockSpec(memory_space=pltpu.VMEM),
        scratch_shapes=[
            pltpu.VMEM((slots, 2, ROWS, HEAD_DIM), BF16),
            pltpu.VMEM((GROUP, ROWS, HEAD_DIM), BF16),
            pltpu.VMEM((GROUP, ROWS, HEAD_DIM), BF16),
            pltpu.VMEM((slots, GROUP, ROWS, ROWS), BF16),
            pltpu.VMEM((slots, GROUP, ROWS, ROWS), BF16),
            pltpu.VMEM((slots, GROUP, 1, ROWS), F32),
            pltpu.VMEM((GROUP, 1, ROWS), F32),
            pltpu.VMEM((GROUP, 1, ROWS), F32),
            pltpu.VMEM((GROUP, 1, ROWS), F32),
            pltpu.VMEM((GROUP, HEAD_DIM, ROWS), F32),
            pltpu.VMEM((HEAD_DIM, ROWS), BF16),
            pltpu.VMEM((2, ROWS, HEAD_DIM), F32),
            pltpu.VMEM((slots, 2, ROWS, HEAD_DIM), BF16),
            pltpu.VMEM((FAR + 1, 2, ROWS, HEAD_DIM), BF16),
            pltpu.VMEM((FAR + 1, 2, ROWS, HEAD_DIM), BF16),
            pltpu.VMEM((ROWS, HEAD_DIM), F32),
            pltpu.VMEM((ROWS, HEAD_DIM), F32),
            dma((GROUP,)),
            dma((GROUP,)),
            dma((2,)),
            dma((FAR + 1,)),
            dma((slots,)),
            dma((FAR + 1,)),
            dma((FAR + 1,)),
            dma((FAR + 1,)),
            dma((FAR + 1,)),
            dma((FAR + 1,)),
        ],
        compiler_params=pltpu.CompilerParams(
            collective_id=0, has_side_effects=True, vmem_limit_bytes=56 * 1024 * 1024
        ),
        name="attention",
    )(q, k, v, g, docs)


LAG = 2


def project_kernel(
    a_ref, wq, wk, wv, out_ref,
    w, px, rx1, sx2, rx2, pz, rz1, sz2, rz2,
    w_sem, x1_send, x1_recv, x2_send, x2_recv, z1_send, z1_recv, z2_send, z2_recv,
):
    t = lax.axis_index("tp")
    z, x = t // 2, t % 2
    base = GROUP * HEAD_DIM

    def loads(i):
        rows = pl.ds(i * WIDTH, WIDTH)
        return [
            pltpu.make_async_copy(wq.at[rows], w.at[rows, 0:base], w_sem.at[i, 0]),
            pltpu.make_async_copy(wk.at[rows], w.at[rows, base:base + HEAD_DIM], w_sem.at[i, 1]),
            pltpu.make_async_copy(wv.at[rows], w.at[rows, base + HEAD_DIM:DEPTH], w_sem.at[i, 2]),
        ]

    for i in range(STEPS):
        for load in loads(i):
            load.start()

    def beside(o):
        return 2 * ((z + o) % 4) + x

    across = t + 1 - 2 * x
    barrier = pltpu.get_barrier_semaphore()
    for other in (across, beside(1), beside(2), beside(3)):
        pl.semaphore_signal(barrier, inc=1, device_id={"tp": other}, device_id_type=pl.DeviceIdType.MESH)
    pl.semaphore_wait(barrier, 4)

    def x1(i):
        return remote(px.at[i, pl.ds((1 - x) * 128, 128)], rx1.at[i], x1_send.at[i], x1_recv.at[i], tp=across)

    def x2(i, o):
        return remote(sx2.at[i, (z + o) % 4], rx2.at[i, o - 1], x2_send.at[i, o - 1], x2_recv.at[i, o - 1], tp=beside(o))

    def z1(i, o):
        return remote(pz.at[i, (z + o) % 4], rz1.at[i, o - 1], z1_send.at[i, o - 1], z1_recv.at[i, o - 1], tp=beside(o))

    def z2(i):
        return remote(sz2.at[i, 1 - x], rz2.at[i], z2_send.at[i], z2_recv.at[i], tp=across)

    def compute(i):
        for load in loads(i):
            load.wait()
        for part in range(2):
            lo, wide = (0, WIDE_X) if part == 0 else (WIDE_X, WIDE_Z)
            product = dot_nt(a_ref[...], w[pl.ds(i * WIDTH + lo, wide), :]).astype(BF16)
            if part == 0:
                px[i] = product
                x1(i).start()
            else:
                for to in range(4):
                    for half in range(2):
                        rows = half * 128 + to * 32
                        pz[i, to, half * 32:(half + 1) * 32] = product[rows:rows + 32]
                for o in (2, 1, 3):
                    z1(i, o).start()

    def middle(i):
        x1(i).wait_recv()
        both = rx1[i].astype(F32) + px[i, pl.ds(x * 128, 128)].astype(F32)
        both = both.astype(BF16)
        for to in range(4):
            sx2[i, to] = both[to * 32:(to + 1) * 32]
        for o in (2, 1, 3):
            x2(i, o).start()
        ring = pz[i, z].astype(F32)
        for o in (1, 3, 2):
            z1(i, o).wait_recv()
            ring = ring + rz1[i, o - 1].astype(F32)
        ring = ring.astype(BF16)
        sz2[i, 0] = ring[:32]
        sz2[i, 1] = ring[32:]
        z2(i).start()

    def last(i):
        result = sx2[i, z].astype(F32)
        for o in (1, 3, 2):
            x2(i, o).wait_recv()
            result = result + rx2[i, o - 1].astype(F32)
        out_ref[:, pl.ds(i * WIDTH, WIDE_X)] = result.astype(BF16)
        z2(i).wait_recv()
        result = sz2[i, x].astype(F32) + rz2[i].astype(F32)
        out_ref[:, pl.ds(i * WIDTH + WIDE_X, WIDE_Z)] = result.astype(BF16)

    def step(i, carry):
        @pl.when(i < STEPS)
        def _():
            compute(i)

        @pl.when((i >= LAG) & (i < STEPS + LAG))
        def _():
            middle(i - LAG)

        @pl.when(i >= 2 * LAG)
        def _():
            last(i - 2 * LAG)

        return carry

    lax.fori_loop(0, STEPS + 2 * LAG, step, 0)

    def drain(i, carry):
        x1(i).wait_send()
        z2(i).wait_send()
        for o in (1, 2, 3):
            x2(i, o).wait_send()
            z1(i, o).wait_send()
        return carry

    lax.fori_loop(0, STEPS, drain, 0)


def project(a, wq, wk, wv):
    any_spec = pl.BlockSpec(memory_space=pl.ANY)
    vmem = pl.BlockSpec(memory_space=pltpu.VMEM)
    dma = pltpu.SemaphoreType.DMA
    width = wq.shape[0]
    return pl.pallas_call(
        project_kernel,
        out_shape=jax.ShapeDtypeStruct((ROWS // 8, width), BF16),
        in_specs=[vmem] + [any_spec] * 3,
        out_specs=vmem,
        scratch_shapes=[
            pltpu.VMEM((width, DEPTH), BF16),
            pltpu.VMEM((STEPS, ROWS, WIDE_X), BF16),
            pltpu.VMEM((STEPS, 128, WIDE_X), BF16),
            pltpu.VMEM((STEPS, 4, 32, WIDE_X), BF16),
            pltpu.VMEM((STEPS, 3, 32, WIDE_X), BF16),
            pltpu.VMEM((STEPS, 4, 64, WIDE_Z), BF16),
            pltpu.VMEM((STEPS, 3, 64, WIDE_Z), BF16),
            pltpu.VMEM((STEPS, 2, 32, WIDE_Z), BF16),
            pltpu.VMEM((STEPS, 32, WIDE_Z), BF16),
            dma((STEPS, 3)),
            dma((STEPS,)),
            dma((STEPS,)),
            dma((STEPS, 3)),
            dma((STEPS, 3)),
            dma((STEPS, 3)),
            dma((STEPS, 3)),
            dma((STEPS,)),
            dma((STEPS,)),
        ],
        compiler_params=pltpu.CompilerParams(
            collective_id=1, has_side_effects=True, vmem_limit_bytes=56 * 1024 * 1024
        ),
        name="project",
    )(a, wq, wk, wv)


def local(query_rows, key_rows, value_rows, grad_out, doc_ids, w_query, w_key, w_value):
    a = attention(query_rows, key_rows, value_rows, grad_out, doc_ids)
    return project(a, w_query, w_key, w_value)


def solution(mesh):
    in_specs = (
        P("ctx", "tp"),
        P("ctx", "tp"),
        P("ctx", "tp"),
        P("ctx", "tp"),
        P(),
        P(None, "tp"),
        P(None, "tp"),
        P(None, "tp"),
    )
    out_specs = P(("ctx", "tp"), None)
    return jax.shard_map(local, mesh=mesh, in_specs=in_specs, out_specs=out_specs, check_vma=False)
```

```python
import functools
import math

import jax
import jax.numpy as jnp
from jax import lax
from jax.experimental import pallas as pl
from jax.experimental.pallas import tpu as pltpu
from jax.sharding import PartitionSpec as P

HEADS = 64
KV_HEADS = 8
HEAD_DIM = 128
BLK = 128
GROUP = HEADS // KV_HEADS
BLOCKS = 32
THETA = 500000.0
NEGATIVE = -1e30
ROWS = 256
FAR = 4
SCALE = HEAD_DIM ** (-0.5)
LOG2_SCALE = SCALE * math.log2(math.e)
STEPS = 8
WIDTH = 1024
WIDE = WIDTH // 2
RING = 3
LAG = 1
DEPTH = GROUP * HEAD_DIM + 2 * HEAD_DIM
F32 = jnp.float32
BF16 = jnp.bfloat16


def dot_nt(left, right):
    return lax.dot_general(left, right, (((1,), (1,)), ((), ())), preferred_element_type=F32)


def dot_nn(left, right):
    return lax.dot_general(left, right, (((1,), (0,)), ((), ())), preferred_element_type=F32)


def remote(src, dst, send, recv, **device):
    return pltpu.make_async_remote_copy(
        src_ref=src, dst_ref=dst, send_sem=send, recv_sem=recv,
        device_id=device, device_id_type=pl.DeviceIdType.MESH,
    )


def layer_kernel(
    q_hbm, k_hbm, v_hbm, g_hbm, docs, wq, wk, wv, out_ref,
    kv, qs, gs, ws, gps, far_ws, far_gps, tops, top, total, weighted, dqt, kt, acc, stage, pair, back, cosine, sine,
    a_ref, w, s1, r1, s2, r2, s3, r3,
    q_sem, g_sem, own_sem, kv_send, kv_recv, pass_send, pair_send, pair_recv, back_send, back_recv,
    w_sem, s1_send, s1_recv, s2_send, s2_recv, s3_send, s3_recv,
):
    c = lax.axis_index("ctx")
    size = lax.axis_size("ctx")
    chips = size // 2
    chip, core = c // 2, c % 2
    sibling = c + 1 - 2 * core

    q_loads = [pltpu.make_async_copy(q_hbm.at[:, pl.ds(h * HEAD_DIM, HEAD_DIM)], qs.at[h], q_sem.at[h]) for h in range(GROUP)]
    g_loads = [pltpu.make_async_copy(g_hbm.at[:, pl.ds(h * HEAD_DIM, HEAD_DIM)], gs.at[h], g_sem.at[h]) for h in range(GROUP)]
    own_loads = [pltpu.make_async_copy(k_hbm, kv.at[0, 0], own_sem.at[0]), pltpu.make_async_copy(v_hbm, kv.at[0, 1], own_sem.at[1])]
    for load in own_loads + q_loads + g_loads:
        load.start()

    t = lax.axis_index("tp")
    z, x = t // 2, t % 2
    across = t + 1 - 2 * x
    z_pairs = (2 * (z + 1 - 2 * (z % 2)) + x, 2 * (3 - z) + x)

    base = GROUP * HEAD_DIM

    def loads(i):
        rows = pl.ds(i * WIDTH, WIDTH)
        slot = i % RING
        return [
            pltpu.make_async_copy(wq.at[rows], w.at[slot, :, 0:base], w_sem.at[slot, 0]),
            pltpu.make_async_copy(wk.at[rows], w.at[slot, :, base:base + HEAD_DIM], w_sem.at[slot, 1]),
            pltpu.make_async_copy(wv.at[rows], w.at[slot, :, base + HEAD_DIM:DEPTH], w_sem.at[slot, 2]),
        ]

    for i in range(RING - 1):
        for load in loads(i):
            load.start()

    barrier = pltpu.get_barrier_semaphore()
    pl.semaphore_signal(barrier, inc=1, device_id={"ctx": sibling}, device_id_type=pl.DeviceIdType.MESH)
    for m in range(1, chips):
        pl.semaphore_signal(barrier, inc=1, device_id={"ctx": (c + 2 * m) % size}, device_id_type=pl.DeviceIdType.MESH)
    for other in (across,) + z_pairs:
        pl.semaphore_signal(barrier, inc=1, device_id={"tp": other}, device_id_type=pl.DeviceIdType.MESH)
    pl.semaphore_wait(barrier, chips + 3)

    for load in own_loads:
        load.wait()

    def key_copy(m):
        return remote(kv.at[0], kv.at[2 * m], kv_send.at[m], kv_recv.at[2 * m], ctx=(c + 2 * m) % size)

    def pass_copy(m):
        slot = 2 * m + 1 - 2 * core
        return remote(kv.at[2 * m], kv.at[slot], pass_send.at[m], kv_recv.at[slot], ctx=sibling)

    def passes(m):
        return (chip >= m) & ((m > 0) | (core == 0)) & ((m < FAR) | (core == 1))

    @pl.when(core == 0)
    def _():
        pass_copy(0).start()

    for m in range(1, FAR + 1):
        @pl.when(chip + m < chips)
        def _():
            key_copy(m).start()

    places = (c * ROWS + lax.broadcasted_iota(jnp.int32, (ROWS, HEAD_DIM), 0)).astype(F32)
    lanes = lax.broadcasted_iota(jnp.int32, (ROWS, HEAD_DIM), 1)
    half = HEAD_DIM // 2
    pair_lane = jnp.where(lanes < half, lanes, lanes - half).astype(F32)
    angles = places * jnp.exp(pair_lane * (-2.0 * math.log(THETA) / HEAD_DIM))
    cosine[...] = jnp.cos(angles)
    sine[...] = jnp.where(lanes < half, 1.0, -1.0) * jnp.sin(angles)

    def rope_back(y):
        return y * cosine[...] + pltpu.roll(y, half, 1) * sine[...]

    starts = []
    for block in range(2):
        document = docs[2 * c + block]
        starts.append(sum([(docs[b] < document).astype(jnp.int32) for b in range(BLOCKS)]))
    lane = lax.broadcasted_iota(jnp.int32, (1, ROWS), 1)
    start_row = jnp.where(lane < BLK, starts[0], starts[1])

    dqt[...] = jnp.zeros_like(dqt)
    for load in q_loads + g_loads:
        load.wait()

    key_at = lax.broadcasted_iota(jnp.int32, (ROWS, ROWS), 0)
    query_at = lax.broadcasted_iota(jnp.int32, (ROWS, ROWS), 1)
    far = 2 * FAR

    def shifted_exp(s, row, bias):
        return jnp.concatenate(
            [jnp.exp2(s[b * BLK:(b + 1) * BLK] * LOG2_SCALE - (row - bias[b])) for b in range(2)], axis=0
        )

    def tile_stats(d, first):
        key_block = 2 * (c - d)
        bias = [jnp.where(key_block + b >= start_row, 0.0, NEGATIVE) for b in range(2)]
        for h in range(GROUP):
            s = dot_nt(kv[d, 0], qs[h])
            gp = dot_nt(kv[d, 1], gs[h])
            gps[d, h] = gp
            if first:
                s = jnp.where(key_at <= query_at, s, NEGATIVE)
            new = jnp.maximum(*[
                jnp.max(s[b * BLK:(b + 1) * BLK], axis=0, keepdims=True) * LOG2_SCALE + bias[b] for b in range(2)
            ])
            if not first:
                old = top[h]
                new = jnp.maximum(old, new)
            w = shifted_exp(s, new, bias)
            part = jnp.sum(w, axis=0, keepdims=True)
            part_weighted = jnp.sum(w * gp, axis=0, keepdims=True)
            if not first:
                factor = jnp.exp2(old - new)
                part = total[h] * factor + part
                part_weighted = weighted[h] * factor + part_weighted
            top[h] = new
            tops[d, h] = new
            total[h] = part
            weighted[h] = part_weighted
            ws[d, h] = w.astype(BF16)

    def far_stats():
        bias = jnp.where(2 * (c - far) + 1 >= starts[0], 0.0, NEGATIVE)
        for h in range(GROUP):
            s = dot_nt(kv[far, 0, BLK:], qs[h, :BLK])
            gp = dot_nt(kv[far, 1, BLK:], gs[h, :BLK])
            old = top[h, :, :BLK]
            new = jnp.maximum(old, jnp.max(s, axis=0, keepdims=True) * LOG2_SCALE + bias)
            w = jnp.exp2(s * LOG2_SCALE - (new - bias))
            factor = jnp.exp2(old - new)
            top[h, :, :BLK] = new
            tops[far, h, :, :BLK] = new
            total[h, :, :BLK] = total[h, :, :BLK] * factor + jnp.sum(w, axis=0, keepdims=True)
            weighted[h, :, :BLK] = weighted[h, :, :BLK] * factor + jnp.sum(w * gp, axis=0, keepdims=True)
            far_ws[h] = w.astype(BF16)
            far_gps[h] = gp

    tile_stats(0, True)

    def near(d, carry):
        m = (d + 1) // 2

        @pl.when((d % 2 == 1) & (chip >= m))
        def _():
            key_copy(m).wait_recv()

            @pl.when(passes(m))
            def _():
                pass_copy(m).start()

        @pl.when(c >= d)
        def _():
            @pl.when(d % 2 == 1)
            def _():
                remote(kv.at[d], kv.at[d], pass_send.at[0], kv_recv.at[d], ctx=sibling).wait_recv()

            tile_stats(d, False)

        return carry

    lax.fori_loop(1, far, near, 0)

    @pl.when(c >= far)
    def _():
        far_stats()

    for h in range(GROUP):
        inverse = 1.0 / total[h]
        total[h] = inverse
        weighted[h] = weighted[h] * inverse

    def tile_grads(d):
        kt[...] = jnp.transpose(kv[d, 0].astype(F32)).astype(BF16)
        key_total = value_total = None
        for h in range(GROUP):
            p = ws[d, h].astype(F32) * (jnp.exp2(tops[d, h] - top[h]) * total[h])
            ds = (p * (gps[d, h] - weighted[h])).astype(BF16)
            if h == 0:
                acc[0] = dot_nn(ds, qs[h])
                acc[1] = dot_nn(p.astype(BF16), gs[h])
            else:
                acc[0] += dot_nn(ds, qs[h])
                acc[1] += dot_nn(p.astype(BF16), gs[h])
            dqt[h] += dot_nn(kt[...], ds)

    def far_grads():
        kt[...] = jnp.transpose(kv[far, 0].astype(F32)).astype(BF16)
        acc[...] = jnp.zeros_like(acc)
        for h in range(GROUP):
            p = far_ws[h].astype(F32) * (jnp.exp2(tops[far, h, :, :BLK] - top[h, :, :BLK]) * total[h, :, :BLK])
            ds = (p * (far_gps[h] - weighted[h, :, :BLK])).astype(BF16)
            acc[0, BLK:] += dot_nn(ds, qs[h, :BLK])
            acc[1, BLK:] += dot_nn(p.astype(BF16), gs[h, :BLK])
            dqt[h, :, :BLK] += dot_nn(kt[:, BLK:], ds)

    def pair_copy(d):
        slot = (d + 1 - 2 * core) // 2
        return remote(stage.at[d], pair.at[slot], pair_send.at[d // 2], pair_recv.at[slot], ctx=sibling)

    def pair_wait(m):
        remote(stage.at[0], pair.at[m], pair_send.at[0], pair_recv.at[m], ctx=sibling).wait_recv()

    def back_copy(m):
        return remote(stage.at[2 * m], back.at[m], back_send.at[m], back_recv.at[m], ctx=(c + size - 2 * m) % size)

    def inward(step, carry):
        m = FAR - step // 2
        d = 2 * m - 1 + step % 2

        @pl.when((d < far) & (c >= d))
        def _():
            tile_grads(d)

        @pl.when((d == far) & (c >= d))
        def _():
            far_grads()

        @pl.when((step % 2 == 0) & (c >= d))
        def _():
            stage[d] = acc[...].astype(BF16)
            pair_copy(d).start()

        @pl.when((step % 2 == 1) & (c >= d))
        def _():
            @pl.when((m < FAR) | (core == 1))
            def _():
                pair_wait(m)
                acc[...] += pair[m].astype(F32)

            stage[d] = acc[...].astype(BF16)
            back_copy(m).start()

        return carry

    lax.fori_loop(0, far, inward, 0)
    tile_grads(0)

    for h in range(GROUP):
        a_ref[:, h * HEAD_DIM:(h + 1) * HEAD_DIM] = rope_back(jnp.transpose(dqt[h]) * SCALE).astype(BF16)

    @pl.when(core == 0)
    def _():
        pair_wait(0)
        acc[...] += pair[0].astype(F32)

    for m in range(FAR, 0, -1):
        @pl.when(chip + m < chips)
        def _():
            back_copy(m).wait_recv()
            acc[...] += back[m].astype(F32)

    a_ref[:, base:base + HEAD_DIM] = rope_back(acc[0] * SCALE).astype(BF16)
    a_ref[:, base + HEAD_DIM:DEPTH] = acc[1].astype(BF16)

    kept_half = (((z + 1) // 2) % 2, z // 2)
    kept_part = (z // 2, z % 2)

    def first_copy(i, kind):
        n = 2 * i + kind
        return remote(s1.at[n, 1 - kept_half[kind]], r1.at[n], s1_send.at[n], s1_recv.at[n], tp=z_pairs[kind])

    def second_copy(i, kind):
        n = 2 * i + kind
        return remote(s2.at[n, 1 - x], r2.at[n], s2_send.at[n], s2_recv.at[n], tp=across)

    def third_copy(i, kind):
        n = 2 * i + kind
        return remote(s3.at[n, 1 - kept_part[kind]], r3.at[n], s3_send.at[n], s3_recv.at[n], tp=z_pairs[1 - kind])

    def compute(i):
        @pl.when(i + RING - 1 < STEPS)
        def _():
            for load in loads(i + RING - 1):
                load.start()

        for load in loads(i):
            load.wait()
        for kind in range(2):
            n = 2 * i + kind
            product = dot_nt(a_ref[...], w[i % RING, kind * WIDE:(kind + 1) * WIDE, :]).astype(BF16)
            for to_z in range(4):
                half = ((to_z + 1) // 2 % 2, to_z // 2)[kind]
                part = (to_z // 2, to_z % 2)[kind]
                for to_x in range(2):
                    rows = to_z * 64 + to_x * 32
                    s1[n, half, to_x * 64 + part * 32:to_x * 64 + part * 32 + 32] = product[rows:rows + 32]
            first_copy(i, kind).start()

    def second(i):
        for kind in range(2):
            n = 2 * i + kind
            first_copy(i, kind).wait_recv()
            value = (s1[n, kept_half[kind]].astype(F32) + r1[n].astype(F32)).astype(BF16)
            s2[n, 0] = value[:64]
            s2[n, 1] = value[64:]
            second_copy(i, kind).start()

    def third(i):
        for kind in range(2):
            n = 2 * i + kind
            second_copy(i, kind).wait_recv()
            value = (s2[n, x].astype(F32) + r2[n].astype(F32)).astype(BF16)
            s3[n, 0] = value[:32]
            s3[n, 1] = value[32:]
            third_copy(i, kind).start()

    def last(i):
        for kind in range(2):
            n = 2 * i + kind
            third_copy(i, kind).wait_recv()
            value = s3[n, kept_part[kind]].astype(F32) + r3[n].astype(F32)
            out_ref[:, pl.ds(i * WIDTH + kind * WIDE, WIDE)] = value.astype(BF16)

    def step(i, carry):
        @pl.when(i < STEPS)
        def _():
            compute(i)

        for number, work in enumerate((second, third, last)):
            lag = (number + 1) * LAG

            @pl.when((i >= lag) & (i < STEPS + lag))
            def _():
                work(i - lag)

        return carry

    lax.fori_loop(0, STEPS + 3 * LAG, step, 0)

    def drain(i, carry):
        for kind in range(2):
            first_copy(i, kind).wait_send()
            second_copy(i, kind).wait_send()
            third_copy(i, kind).wait_send()
        return carry

    lax.fori_loop(0, STEPS, drain, 0)

    for m in range(FAR + 1):
        @pl.when(passes(m))
        def _():
            pass_copy(m).wait_send()

    for m in range(1, FAR + 1):
        @pl.when(chip + m < chips)
        def _():
            key_copy(m).wait_send()

        @pl.when(c >= 2 * m - 1)
        def _():
            pair_copy(2 * m - 1).wait_send()

        @pl.when(chip >= m)
        def _():
            back_copy(m).wait_send()


def layer(q, k, v, g, docs, wq, wk, wv):
    any_spec = pl.BlockSpec(memory_space=pl.ANY)
    slots = 2 * FAR + 1
    dma = pltpu.SemaphoreType.DMA
    width = wq.shape[0]
    chunks = 2 * STEPS
    return pl.pallas_call(
        layer_kernel,
        out_shape=jax.ShapeDtypeStruct((ROWS // 8, width), BF16),
        in_specs=[any_spec] * 4 + [pl.BlockSpec(memory_space=pltpu.SMEM)] + [any_spec] * 3,
        out_specs=pl.BlockSpec(memory_space=pltpu.VMEM),
        scratch_shapes=[
            pltpu.VMEM((slots, 2, ROWS, HEAD_DIM), BF16),
            pltpu.VMEM((GROUP, ROWS, HEAD_DIM), BF16),
            pltpu.VMEM((GROUP, ROWS, HEAD_DIM), BF16),
            pltpu.VMEM((slots - 1, GROUP, ROWS, ROWS), BF16),
            pltpu.VMEM((slots - 1, GROUP, ROWS, ROWS), F32),
            pltpu.VMEM((GROUP, BLK, BLK), BF16),
            pltpu.VMEM((GROUP, BLK, BLK), F32),
            pltpu.VMEM((slots, GROUP, 1, ROWS), F32),
            pltpu.VMEM((GROUP, 1, ROWS), F32),
            pltpu.VMEM((GROUP, 1, ROWS), F32),
            pltpu.VMEM((GROUP, 1, ROWS), F32),
            pltpu.VMEM((GROUP, HEAD_DIM, ROWS), F32),
            pltpu.VMEM((HEAD_DIM, ROWS), BF16),
            pltpu.VMEM((2, ROWS, HEAD_DIM), F32),
            pltpu.VMEM((slots, 2, ROWS, HEAD_DIM), BF16),
            pltpu.VMEM((FAR + 1, 2, ROWS, HEAD_DIM), BF16),
            pltpu.VMEM((FAR + 1, 2, ROWS, HEAD_DIM), BF16),
            pltpu.VMEM((ROWS, HEAD_DIM), F32),
            pltpu.VMEM((ROWS, HEAD_DIM), F32),
            pltpu.VMEM((ROWS, DEPTH), BF16),
            pltpu.VMEM((RING, WIDTH, DEPTH), BF16),
            pltpu.VMEM((chunks, 2, 128, WIDE), BF16),
            pltpu.VMEM((chunks, 128, WIDE), BF16),
            pltpu.VMEM((chunks, 2, 64, WIDE), BF16),
            pltpu.VMEM((chunks, 64, WIDE), BF16),
            pltpu.VMEM((chunks, 2, 32, WIDE), BF16),
            pltpu.VMEM((chunks, 32, WIDE), BF16),
            dma((GROUP,)),
            dma((GROUP,)),
            dma((2,)),
            dma((FAR + 1,)),
            dma((slots,)),
            dma((FAR + 1,)),
            dma((FAR + 1,)),
            dma((FAR + 1,)),
            dma((FAR + 1,)),
            dma((FAR + 1,)),
            dma((RING, 3)),
        ] + [dma((chunks,))] * 6,
        compiler_params=pltpu.CompilerParams(
            collective_id=0, has_side_effects=True, vmem_limit_bytes=60 * 1024 * 1024
        ),
        name="layer",
    )(q, k, v, g, docs, wq, wk, wv)


def local(query_rows, key_rows, value_rows, grad_out, doc_ids, w_query, w_key, w_value):
    return layer(query_rows, key_rows, value_rows, grad_out, doc_ids, w_query, w_key, w_value)


def solution(mesh):
    in_specs = (
        P("ctx", "tp"),
        P("ctx", "tp"),
        P("ctx", "tp"),
        P("ctx", "tp"),
        P(),
        P(None, "tp"),
        P(None, "tp"),
        P(None, "tp"),
    )
    out_specs = P(("ctx", "tp"), None)
    return jax.shard_map(local, mesh=mesh, in_specs=in_specs, out_specs=out_specs, check_vma=False)
```

```python
import functools
import math

import jax
import jax.numpy as jnp
from jax import lax
from jax.experimental import pallas as pl
from jax.experimental.pallas import tpu as pltpu
from jax.sharding import PartitionSpec as P

HEADS = 64
KV_HEADS = 8
HEAD_DIM = 128
BLK = 128
GROUP = HEADS // KV_HEADS
BLOCKS = 32
THETA = 500000.0
NEGATIVE = -1e30
ROWS = 256
FAR = 4
SCALE = HEAD_DIM ** (-0.5)
LOG2_SCALE = SCALE * math.log2(math.e)
STEPS = 8
WIDTH = 1024
WIDE = WIDTH // 2
RING = 3
LAG = 3
X_STEP = 1
DEPTH = GROUP * HEAD_DIM + 2 * HEAD_DIM
F32 = jnp.float32
BF16 = jnp.bfloat16


def dot_nt(left, right):
    return lax.dot_general(left, right, (((1,), (1,)), ((), ())), preferred_element_type=F32)


def dot_nn(left, right):
    return lax.dot_general(left, right, (((1,), (0,)), ((), ())), preferred_element_type=F32)


def remote(src, dst, send, recv, **device):
    return pltpu.make_async_remote_copy(
        src_ref=src, dst_ref=dst, send_sem=send, recv_sem=recv,
        device_id=device, device_id_type=pl.DeviceIdType.MESH,
    )


def layer_kernel(
    q_hbm, k_hbm, v_hbm, g_hbm, docs, wq, wk, wv, out_ref,
    kv, qs, gs, ws, gps, far_ws, far_gps, tops, top, total, weighted, dqt, kt, acc, stage, pair, back, cosine, sine,
    a_ref, w, s1, r1, s2, r2, s3, r3,
    q_sem, g_sem, own_sem, kv_send, kv_recv, pass_send, pair_send, pair_recv, back_send, back_recv,
    w_sem, s1_send, s1_recv, s2_send, s2_recv, s3_send, s3_recv,
):
    c = lax.axis_index("ctx")
    size = lax.axis_size("ctx")
    chips = size // 2
    chip, core = c // 2, c % 2
    sibling = c + 1 - 2 * core

    q_loads = [pltpu.make_async_copy(q_hbm.at[:, pl.ds(h * HEAD_DIM, HEAD_DIM)], qs.at[h], q_sem.at[h]) for h in range(GROUP)]
    g_loads = [pltpu.make_async_copy(g_hbm.at[:, pl.ds(h * HEAD_DIM, HEAD_DIM)], gs.at[h], g_sem.at[h]) for h in range(GROUP)]
    own_loads = [pltpu.make_async_copy(k_hbm, kv.at[0, 0], own_sem.at[0]), pltpu.make_async_copy(v_hbm, kv.at[0, 1], own_sem.at[1])]
    for load in own_loads + q_loads + g_loads:
        load.start()

    t = lax.axis_index("tp")
    z, x = t // 2, t % 2
    across = t + 1 - 2 * x
    z_pairs = (2 * (z + 1 - 2 * (z % 2)) + x, 2 * (3 - z) + x)

    base = GROUP * HEAD_DIM

    def loads(i):
        rows = pl.ds(i * WIDTH, WIDTH)
        slot = i % RING
        return [
            pltpu.make_async_copy(wq.at[rows], w.at[slot, :, 0:base], w_sem.at[slot, 0]),
            pltpu.make_async_copy(wk.at[rows], w.at[slot, :, base:base + HEAD_DIM], w_sem.at[slot, 1]),
            pltpu.make_async_copy(wv.at[rows], w.at[slot, :, base + HEAD_DIM:DEPTH], w_sem.at[slot, 2]),
        ]

    for i in range(RING - 1):
        for load in loads(i):
            load.start()

    barrier = pltpu.get_barrier_semaphore()
    pl.semaphore_signal(barrier, inc=1, device_id={"ctx": sibling}, device_id_type=pl.DeviceIdType.MESH)
    for m in range(1, chips):
        pl.semaphore_signal(barrier, inc=1, device_id={"ctx": (c + 2 * m) % size}, device_id_type=pl.DeviceIdType.MESH)
    for other in (across,) + z_pairs:
        pl.semaphore_signal(barrier, inc=1, device_id={"tp": other}, device_id_type=pl.DeviceIdType.MESH)
    pl.semaphore_wait(barrier, chips + 3)

    for load in own_loads:
        load.wait()

    def key_copy(m):
        return remote(kv.at[0], kv.at[2 * m], kv_send.at[m], kv_recv.at[2 * m], ctx=(c + 2 * m) % size)

    def pass_copy(m):
        slot = 2 * m + 1 - 2 * core
        return remote(kv.at[2 * m], kv.at[slot], pass_send.at[m], kv_recv.at[slot], ctx=sibling)

    def passes(m):
        return (chip >= m) & ((m > 0) | (core == 0)) & ((m < FAR) | (core == 1))

    @pl.when(core == 0)
    def _():
        pass_copy(0).start()

    for m in range(1, FAR + 1):
        @pl.when(chip + m < chips)
        def _():
            key_copy(m).start()

    places = (c * ROWS + lax.broadcasted_iota(jnp.int32, (ROWS, HEAD_DIM), 0)).astype(F32)
    lanes = lax.broadcasted_iota(jnp.int32, (ROWS, HEAD_DIM), 1)
    half = HEAD_DIM // 2
    pair_lane = jnp.where(lanes < half, lanes, lanes - half).astype(F32)
    angles = places * jnp.exp(pair_lane * (-2.0 * math.log(THETA) / HEAD_DIM))
    cosine[...] = jnp.cos(angles)
    sine[...] = jnp.where(lanes < half, 1.0, -1.0) * jnp.sin(angles)

    def rope_back(y):
        return y * cosine[...] + pltpu.roll(y, half, 1) * sine[...]

    starts = []
    for block in range(2):
        document = docs[2 * c + block]
        starts.append(sum([(docs[b] < document).astype(jnp.int32) for b in range(BLOCKS)]))
    lane = lax.broadcasted_iota(jnp.int32, (1, ROWS), 1)
    start_row = jnp.where(lane < BLK, starts[0], starts[1])

    dqt[...] = jnp.zeros_like(dqt)
    for load in q_loads + g_loads:
        load.wait()

    key_at = lax.broadcasted_iota(jnp.int32, (ROWS, ROWS), 0)
    query_at = lax.broadcasted_iota(jnp.int32, (ROWS, ROWS), 1)
    far = 2 * FAR

    def shifted_exp(s, row, bias):
        return jnp.concatenate(
            [jnp.exp2(s[b * BLK:(b + 1) * BLK] * LOG2_SCALE - (row - bias[b])) for b in range(2)], axis=0
        )

    def tile_stats(d, first):
        key_block = 2 * (c - d)
        bias = [jnp.where(key_block + b >= start_row, 0.0, NEGATIVE) for b in range(2)]
        for h in range(GROUP):
            s = dot_nt(kv[d, 0], qs[h])
            gp = dot_nt(kv[d, 1], gs[h])
            gps[d, h] = gp
            if first:
                s = jnp.where(key_at <= query_at, s, NEGATIVE)
            new = jnp.maximum(*[
                jnp.max(s[b * BLK:(b + 1) * BLK], axis=0, keepdims=True) * LOG2_SCALE + bias[b] for b in range(2)
            ])
            if not first:
                old = top[h]
                new = jnp.maximum(old, new)
            w = shifted_exp(s, new, bias)
            part = jnp.sum(w, axis=0, keepdims=True)
            part_weighted = jnp.sum(w * gp, axis=0, keepdims=True)
            if not first:
                factor = jnp.exp2(old - new)
                part = total[h] * factor + part
                part_weighted = weighted[h] * factor + part_weighted
            top[h] = new
            tops[d, h] = new
            total[h] = part
            weighted[h] = part_weighted
            ws[d, h] = w.astype(BF16)

    def far_stats():
        bias = jnp.where(2 * (c - far) + 1 >= starts[0], 0.0, NEGATIVE)
        for h in range(GROUP):
            s = dot_nt(kv[far, 0, BLK:], qs[h, :BLK])
            gp = dot_nt(kv[far, 1, BLK:], gs[h, :BLK])
            old = top[h, :, :BLK]
            new = jnp.maximum(old, jnp.max(s, axis=0, keepdims=True) * LOG2_SCALE + bias)
            w = jnp.exp2(s * LOG2_SCALE - (new - bias))
            factor = jnp.exp2(old - new)
            top[h, :, :BLK] = new
            tops[far, h, :, :BLK] = new
            total[h, :, :BLK] = total[h, :, :BLK] * factor + jnp.sum(w, axis=0, keepdims=True)
            weighted[h, :, :BLK] = weighted[h, :, :BLK] * factor + jnp.sum(w * gp, axis=0, keepdims=True)
            far_ws[h] = w.astype(BF16)
            far_gps[h] = gp

    tile_stats(0, True)

    def near(d, carry):
        m = (d + 1) // 2

        @pl.when((d % 2 == 1) & (chip >= m))
        def _():
            key_copy(m).wait_recv()

            @pl.when(passes(m))
            def _():
                pass_copy(m).start()

        @pl.when(c >= d)
        def _():
            @pl.when(d % 2 == 1)
            def _():
                remote(kv.at[d], kv.at[d], pass_send.at[0], kv_recv.at[d], ctx=sibling).wait_recv()

            tile_stats(d, False)

        return carry

    lax.fori_loop(1, far, near, 0)

    @pl.when(c >= far)
    def _():
        far_stats()

    for h in range(GROUP):
        inverse = 1.0 / total[h]
        total[h] = inverse
        weighted[h] = weighted[h] * inverse

    def tile_grads(d):
        kt[...] = jnp.transpose(kv[d, 0].astype(F32)).astype(BF16)
        key_total = value_total = None
        for h in range(GROUP):
            p = ws[d, h].astype(F32) * (jnp.exp2(tops[d, h] - top[h]) * total[h])
            ds = (p * (gps[d, h] - weighted[h])).astype(BF16)
            if h == 0:
                acc[0] = dot_nn(ds, qs[h])
                acc[1] = dot_nn(p.astype(BF16), gs[h])
            else:
                acc[0] += dot_nn(ds, qs[h])
                acc[1] += dot_nn(p.astype(BF16), gs[h])
            dqt[h] += dot_nn(kt[...], ds)

    def far_grads():
        kt[...] = jnp.transpose(kv[far, 0].astype(F32)).astype(BF16)
        acc[...] = jnp.zeros_like(acc)
        for h in range(GROUP):
            p = far_ws[h].astype(F32) * (jnp.exp2(tops[far, h, :, :BLK] - top[h, :, :BLK]) * total[h, :, :BLK])
            ds = (p * (far_gps[h] - weighted[h, :, :BLK])).astype(BF16)
            acc[0, BLK:] += dot_nn(ds, qs[h, :BLK])
            acc[1, BLK:] += dot_nn(p.astype(BF16), gs[h, :BLK])
            dqt[h, :, :BLK] += dot_nn(kt[:, BLK:], ds)

    def pair_copy(d):
        slot = (d + 1 - 2 * core) // 2
        return remote(stage.at[d], pair.at[slot], pair_send.at[d // 2], pair_recv.at[slot], ctx=sibling)

    def pair_wait(m):
        remote(stage.at[0], pair.at[m], pair_send.at[0], pair_recv.at[m], ctx=sibling).wait_recv()

    def back_copy(m):
        return remote(stage.at[2 * m], back.at[m], back_send.at[m], back_recv.at[m], ctx=(c + size - 2 * m) % size)

    def inward(step, carry):
        m = FAR - step // 2
        d = 2 * m - 1 + step % 2

        @pl.when((d < far) & (c >= d))
        def _():
            tile_grads(d)

        @pl.when((d == far) & (c >= d))
        def _():
            far_grads()

        @pl.when((step % 2 == 0) & (c >= d))
        def _():
            stage[d] = acc[...].astype(BF16)
            pair_copy(d).start()

        @pl.when((step % 2 == 1) & (c >= d))
        def _():
            @pl.when((m < FAR) | (core == 1))
            def _():
                pair_wait(m)
                acc[...] += pair[m].astype(F32)

            stage[d] = acc[...].astype(BF16)
            back_copy(m).start()

        return carry

    lax.fori_loop(0, far, inward, 0)
    tile_grads(0)

    for h in range(GROUP):
        a_ref[:, h * HEAD_DIM:(h + 1) * HEAD_DIM] = rope_back(jnp.transpose(dqt[h]) * SCALE).astype(BF16)

    @pl.when(core == 0)
    def _():
        pair_wait(0)
        acc[...] += pair[0].astype(F32)

    for m in range(FAR, 0, -1):
        @pl.when(chip + m < chips)
        def _():
            back_copy(m).wait_recv()
            acc[...] += back[m].astype(F32)

    a_ref[:, base:base + HEAD_DIM] = rope_back(acc[0] * SCALE).astype(BF16)
    a_ref[:, base + HEAD_DIM:DEPTH] = acc[1].astype(BF16)

    kept_half = (((z + 1) // 2) % 2, z // 2)
    kept_part = (z // 2, z % 2)

    def order(i, kind):
        x_first = i == X_STEP
        half = kept_half[kind]
        return (
            jnp.where(x_first, x, half),
            jnp.where(x_first, half, x),
            jnp.where(x_first, across, z_pairs[kind]),
            jnp.where(x_first, z_pairs[kind], across),
        )

    def first_copy(i, kind):
        n = 2 * i + kind
        kept, _, partner, _ = order(i, kind)
        return remote(s1.at[n, 1 - kept], r1.at[n], s1_send.at[n], s1_recv.at[n], tp=partner)

    def second_copy(i, kind):
        n = 2 * i + kind
        _, kept, _, partner = order(i, kind)
        return remote(s2.at[n, 1 - kept], r2.at[n], s2_send.at[n], s2_recv.at[n], tp=partner)

    def third_copy(i, kind):
        n = 2 * i + kind
        return remote(s3.at[n, 1 - kept_part[kind]], r3.at[n], s3_send.at[n], s3_recv.at[n], tp=z_pairs[1 - kind])

    def compute(i):
        @pl.when(i + RING - 1 < STEPS)
        def _():
            for load in loads(i + RING - 1):
                load.start()

        for load in loads(i):
            load.wait()
        for kind in range(2):
            n = 2 * i + kind
            product = dot_nt(a_ref[...], w[i % RING, kind * WIDE:(kind + 1) * WIDE, :]).astype(BF16)
            for to_z in range(4):
                half = ((to_z + 1) // 2 % 2, to_z // 2)[kind]
                part = (to_z // 2, to_z % 2)[kind]
                for to_x in range(2):
                    rows = to_z * 64 + to_x * 32
                    outer = jnp.where(i == X_STEP, to_x, half)
                    inner = jnp.where(i == X_STEP, half, to_x)
                    to = pl.multiple_of(inner * 64 + part * 32, 32)
                    s1[n, outer, pl.ds(to, 32)] = product[rows:rows + 32]
            first_copy(i, kind).start()

    def second(i):
        for kind in range(2):
            n = 2 * i + kind
            first_copy(i, kind).wait_recv()
            value = (s1[n, order(i, kind)[0]].astype(F32) + r1[n].astype(F32)).astype(BF16)
            s2[n, 0] = value[:64]
            s2[n, 1] = value[64:]
            second_copy(i, kind).start()

    def third(i):
        for kind in range(2):
            n = 2 * i + kind
            second_copy(i, kind).wait_recv()
            value = (s2[n, order(i, kind)[1]].astype(F32) + r2[n].astype(F32)).astype(BF16)
            s3[n, 0] = value[:32]
            s3[n, 1] = value[32:]
            third_copy(i, kind).start()

    def last(i):
        for kind in range(2):
            n = 2 * i + kind
            third_copy(i, kind).wait_recv()
            value = s3[n, kept_part[kind]].astype(F32) + r3[n].astype(F32)
            out_ref[:, pl.ds(i * WIDTH + kind * WIDE, WIDE)] = value.astype(BF16)

    def step(i, carry):
        @pl.when(i < STEPS)
        def _():
            compute(i)

        for number, work in enumerate((second, third, last)):
            lag = (number + 1) * LAG

            @pl.when((i >= lag) & (i < STEPS + lag))
            def _():
                work(i - lag)

        return carry

    lax.fori_loop(0, STEPS + 3 * LAG, step, 0)

    def drain(i, carry):
        for kind in range(2):
            first_copy(i, kind).wait_send()
            second_copy(i, kind).wait_send()
            third_copy(i, kind).wait_send()
        return carry

    lax.fori_loop(0, STEPS, drain, 0)

    for m in range(FAR + 1):
        @pl.when(passes(m))
        def _():
            pass_copy(m).wait_send()

    for m in range(1, FAR + 1):
        @pl.when(chip + m < chips)
        def _():
            key_copy(m).wait_send()

        @pl.when(c >= 2 * m - 1)
        def _():
            pair_copy(2 * m - 1).wait_send()

        @pl.when(chip >= m)
        def _():
            back_copy(m).wait_send()


def layer(q, k, v, g, docs, wq, wk, wv):
    any_spec = pl.BlockSpec(memory_space=pl.ANY)
    slots = 2 * FAR + 1
    dma = pltpu.SemaphoreType.DMA
    width = wq.shape[0]
    chunks = 2 * STEPS
    return pl.pallas_call(
        layer_kernel,
        out_shape=jax.ShapeDtypeStruct((ROWS // 8, width), BF16),
        in_specs=[any_spec] * 4 + [pl.BlockSpec(memory_space=pltpu.SMEM)] + [any_spec] * 3,
        out_specs=pl.BlockSpec(memory_space=pltpu.VMEM),
        scratch_shapes=[
            pltpu.VMEM((slots, 2, ROWS, HEAD_DIM), BF16),
            pltpu.VMEM((GROUP, ROWS, HEAD_DIM), BF16),
            pltpu.VMEM((GROUP, ROWS, HEAD_DIM), BF16),
            pltpu.VMEM((slots - 1, GROUP, ROWS, ROWS), BF16),
            pltpu.VMEM((slots - 1, GROUP, ROWS, ROWS), F32),
            pltpu.VMEM((GROUP, BLK, BLK), BF16),
            pltpu.VMEM((GROUP, BLK, BLK), F32),
            pltpu.VMEM((slots, GROUP, 1, ROWS), F32),
            pltpu.VMEM((GROUP, 1, ROWS), F32),
            pltpu.VMEM((GROUP, 1, ROWS), F32),
            pltpu.VMEM((GROUP, 1, ROWS), F32),
            pltpu.VMEM((GROUP, HEAD_DIM, ROWS), F32),
            pltpu.VMEM((HEAD_DIM, ROWS), BF16),
            pltpu.VMEM((2, ROWS, HEAD_DIM), F32),
            pltpu.VMEM((slots, 2, ROWS, HEAD_DIM), BF16),
            pltpu.VMEM((FAR + 1, 2, ROWS, HEAD_DIM), BF16),
            pltpu.VMEM((FAR + 1, 2, ROWS, HEAD_DIM), BF16),
            pltpu.VMEM((ROWS, HEAD_DIM), F32),
            pltpu.VMEM((ROWS, HEAD_DIM), F32),
            pltpu.VMEM((ROWS, DEPTH), BF16),
            pltpu.VMEM((RING, WIDTH, DEPTH), BF16),
            pltpu.VMEM((chunks, 2, 128, WIDE), BF16),
            pltpu.VMEM((chunks, 128, WIDE), BF16),
            pltpu.VMEM((chunks, 2, 64, WIDE), BF16),
            pltpu.VMEM((chunks, 64, WIDE), BF16),
            pltpu.VMEM((chunks, 2, 32, WIDE), BF16),
            pltpu.VMEM((chunks, 32, WIDE), BF16),
            dma((GROUP,)),
            dma((GROUP,)),
            dma((2,)),
            dma((FAR + 1,)),
            dma((slots,)),
            dma((FAR + 1,)),
            dma((FAR + 1,)),
            dma((FAR + 1,)),
            dma((FAR + 1,)),
            dma((FAR + 1,)),
            dma((RING, 3)),
        ] + [dma((chunks,))] * 6,
        compiler_params=pltpu.CompilerParams(
            collective_id=0, has_side_effects=True, vmem_limit_bytes=60 * 1024 * 1024
        ),
        name="layer",
    )(q, k, v, g, docs, wq, wk, wv)


def local(query_rows, key_rows, value_rows, grad_out, doc_ids, w_query, w_key, w_value):
    return layer(query_rows, key_rows, value_rows, grad_out, doc_ids, w_query, w_key, w_value)


def solution(mesh):
    in_specs = (
        P("ctx", "tp"),
        P("ctx", "tp"),
        P("ctx", "tp"),
        P("ctx", "tp"),
        P(),
        P(None, "tp"),
        P(None, "tp"),
        P(None, "tp"),
    )
    out_specs = P(("ctx", "tp"), None)
    return jax.shard_map(local, mesh=mesh, in_specs=in_specs, out_specs=out_specs, check_vma=False)
```

```python
import functools
import math

import jax
import jax.numpy as jnp
from jax import lax
from jax.experimental import pallas as pl
from jax.experimental.pallas import tpu as pltpu
from jax.sharding import PartitionSpec as P

HEADS = 64
KV_HEADS = 8
HEAD_DIM = 128
BLK = 128
GROUP = HEADS // KV_HEADS
BLOCKS = 32
THETA = 500000.0
NEGATIVE = -1e30
ROWS = 256
FAR = 4
SCALE = HEAD_DIM ** (-0.5)
LOG2_SCALE = SCALE * math.log2(math.e)
STEPS = 8
WIDTH = 1024
WIDE = WIDTH // 2
RING = 3
LAG = 3
X_STEP = 1
DEPTH = GROUP * HEAD_DIM + 2 * HEAD_DIM
F32 = jnp.float32
BF16 = jnp.bfloat16


def dot_nt(left, right):
    return lax.dot_general(left, right, (((1,), (1,)), ((), ())), preferred_element_type=F32)


def dot_nn(left, right):
    return lax.dot_general(left, right, (((1,), (0,)), ((), ())), preferred_element_type=F32)


def remote(src, dst, send, recv, **device):
    return pltpu.make_async_remote_copy(
        src_ref=src, dst_ref=dst, send_sem=send, recv_sem=recv,
        device_id=device, device_id_type=pl.DeviceIdType.MESH,
    )


def layer_kernel(
    q_hbm, k_hbm, v_hbm, g_hbm, docs, wq, wk, wv, out_ref,
    kv, qs, gs, ws, gps, far_ws, far_gps, tops, top, total, weighted, dqt, kt, far_kt, acc, stage, pair, back, cosine, sine,
    a_ref, w, s1, r1, s2, r2, s3, r3,
    q_sem, g_sem, own_sem, kv_send, kv_recv, pass_send, pair_send, pair_recv, back_send, back_recv,
    w_sem, s1_send, s1_recv, s2_send, s2_recv, s3_send, s3_recv,
):
    c = lax.axis_index("ctx")
    size = lax.axis_size("ctx")
    chips = size // 2
    chip, core = c // 2, c % 2
    sibling = c + 1 - 2 * core

    q_loads = [pltpu.make_async_copy(q_hbm.at[:, pl.ds(h * HEAD_DIM, HEAD_DIM)], qs.at[h], q_sem.at[h]) for h in range(GROUP)]
    g_loads = [pltpu.make_async_copy(g_hbm.at[:, pl.ds(h * HEAD_DIM, HEAD_DIM)], gs.at[h], g_sem.at[h]) for h in range(GROUP)]
    own_loads = [pltpu.make_async_copy(k_hbm, kv.at[0, 0], own_sem.at[0]), pltpu.make_async_copy(v_hbm, kv.at[0, 1], own_sem.at[1])]
    for load in own_loads + q_loads + g_loads:
        load.start()

    t = lax.axis_index("tp")
    z, x = t // 2, t % 2
    across = t + 1 - 2 * x
    z_pairs = (2 * (z + 1 - 2 * (z % 2)) + x, 2 * (3 - z) + x)

    base = GROUP * HEAD_DIM

    def loads(i):
        rows = pl.ds(i * WIDTH, WIDTH)
        slot = i % RING
        return [
            pltpu.make_async_copy(wq.at[rows], w.at[slot, :, 0:base], w_sem.at[slot, 0]),
            pltpu.make_async_copy(wk.at[rows], w.at[slot, :, base:base + HEAD_DIM], w_sem.at[slot, 1]),
            pltpu.make_async_copy(wv.at[rows], w.at[slot, :, base + HEAD_DIM:DEPTH], w_sem.at[slot, 2]),
        ]

    for i in range(RING - 1):
        for load in loads(i):
            load.start()

    barrier = pltpu.get_barrier_semaphore()
    pl.semaphore_signal(barrier, inc=1, device_id={"ctx": sibling}, device_id_type=pl.DeviceIdType.MESH)
    for m in range(1, chips):
        pl.semaphore_signal(barrier, inc=1, device_id={"ctx": (c + 2 * m) % size}, device_id_type=pl.DeviceIdType.MESH)
    for other in (across,) + z_pairs:
        pl.semaphore_signal(barrier, inc=1, device_id={"tp": other}, device_id_type=pl.DeviceIdType.MESH)
    pl.semaphore_wait(barrier, chips + 3)

    for load in own_loads:
        load.wait()

    def key_copy(m):
        return remote(kv.at[0], kv.at[2 * m], kv_send.at[m], kv_recv.at[2 * m], ctx=(c + 2 * m) % size)

    def pass_copy(m):
        slot = 2 * m + 1 - 2 * core
        return remote(kv.at[2 * m], kv.at[slot], pass_send.at[m], kv_recv.at[slot], ctx=sibling)

    def passes(m):
        return (chip >= m) & ((m > 0) | (core == 0)) & ((m < FAR) | (core == 1))

    @pl.when(core == 0)
    def _():
        pass_copy(0).start()

    for m in range(1, FAR + 1):
        @pl.when(chip + m < chips)
        def _():
            key_copy(m).start()

    places = (c * ROWS + lax.broadcasted_iota(jnp.int32, (ROWS, HEAD_DIM), 0)).astype(F32)
    lanes = lax.broadcasted_iota(jnp.int32, (ROWS, HEAD_DIM), 1)
    half = HEAD_DIM // 2
    pair_lane = jnp.where(lanes < half, lanes, lanes - half).astype(F32)
    angles = places * jnp.exp(pair_lane * (-2.0 * math.log(THETA) / HEAD_DIM))
    cosine[...] = jnp.cos(angles)
    sine[...] = jnp.where(lanes < half, 1.0, -1.0) * jnp.sin(angles)

    def rope_back(y):
        return y * cosine[...] + pltpu.roll(y, half, 1) * sine[...]

    starts = []
    for block in range(2):
        document = docs[2 * c + block]
        starts.append(sum([(docs[b] < document).astype(jnp.int32) for b in range(BLOCKS)]))
    lane = lax.broadcasted_iota(jnp.int32, (1, ROWS), 1)
    start_row = jnp.where(lane < BLK, starts[0], starts[1])

    dqt[...] = jnp.zeros_like(dqt)
    for load in q_loads + g_loads:
        load.wait()

    key_at = lax.broadcasted_iota(jnp.int32, (ROWS, ROWS), 0)
    query_at = lax.broadcasted_iota(jnp.int32, (ROWS, ROWS), 1)
    far = 2 * FAR

    def shifted_exp(s, row, bias):
        return jnp.concatenate(
            [jnp.exp2(s[b * BLK:(b + 1) * BLK] * LOG2_SCALE - (row - bias[b])) for b in range(2)], axis=0
        )

    def tile_stats(d, first):
        key_block = 2 * (c - d)
        bias = [jnp.where(key_block + b >= start_row, 0.0, NEGATIVE) for b in range(2)]
        for h in range(GROUP):
            s = dot_nt(kv[d, 0], qs[h])
            gp = dot_nt(kv[d, 1], gs[h])
            gps[d, h] = gp
            if first:
                s = jnp.where(key_at <= query_at, s, NEGATIVE)
            new = jnp.maximum(*[
                jnp.max(s[b * BLK:(b + 1) * BLK], axis=0, keepdims=True) * LOG2_SCALE + bias[b] for b in range(2)
            ])
            if not first:
                old = top[h]
                new = jnp.maximum(old, new)
            halves = [jnp.exp2(s[b * BLK:(b + 1) * BLK] * LOG2_SCALE - (new - bias[b])) for b in range(2)]
            part = jnp.sum(halves[0] + halves[1], axis=0, keepdims=True)
            part_weighted = jnp.sum(halves[0] * gp[:BLK] + halves[1] * gp[BLK:], axis=0, keepdims=True)
            if not first:
                factor = jnp.exp2(old - new)
                part = total[h] * factor + part
                part_weighted = weighted[h] * factor + part_weighted
            top[h] = new
            tops[d, h] = new
            total[h] = part
            weighted[h] = part_weighted
            for b in range(2):
                ws[h, d, b * BLK:(b + 1) * BLK] = halves[b].astype(BF16)

    def far_stats():
        bias = jnp.where(2 * (c - far) + 1 >= starts[0], 0.0, NEGATIVE)
        for h in range(GROUP):
            s = dot_nt(kv[far, 0, BLK:], qs[h, :BLK])
            gp = dot_nt(kv[far, 1, BLK:], gs[h, :BLK])
            old = top[h, :, :BLK]
            new = jnp.maximum(old, jnp.max(s, axis=0, keepdims=True) * LOG2_SCALE + bias)
            w = jnp.exp2(s * LOG2_SCALE - (new - bias))
            factor = jnp.exp2(old - new)
            top[h, :, :BLK] = new
            tops[far, h, :, :BLK] = new
            total[h, :, :BLK] = total[h, :, :BLK] * factor + jnp.sum(w, axis=0, keepdims=True)
            weighted[h, :, :BLK] = weighted[h, :, :BLK] * factor + jnp.sum(w * gp, axis=0, keepdims=True)
            far_ws[h] = w.astype(BF16)
            far_gps[h] = gp

    tile_stats(0, True)
    kt[:, :ROWS] = jnp.transpose(kv[0, 0].astype(F32)).astype(BF16)

    def near(d, carry):
        m = (d + 1) // 2

        @pl.when((d % 2 == 1) & (chip >= m))
        def _():
            key_copy(m).wait_recv()

            @pl.when(passes(m))
            def _():
                pass_copy(m).start()

        @pl.when(c >= d)
        def _():
            @pl.when(d % 2 == 1)
            def _():
                remote(kv.at[d], kv.at[d], pass_send.at[0], kv_recv.at[d], ctx=sibling).wait_recv()

            tile_stats(d, False)
            kt[:, pl.ds(pl.multiple_of(d * ROWS, ROWS), ROWS)] = jnp.transpose(kv[d, 0].astype(F32)).astype(BF16)

        @pl.when(c < d)
        def _():
            kt[:, pl.ds(pl.multiple_of(d * ROWS, ROWS), ROWS)] = jnp.zeros((HEAD_DIM, ROWS), BF16)
            for h in range(GROUP):
                ws[h, d] = jnp.zeros((ROWS, ROWS), BF16)

        return carry

    lax.fori_loop(1, far, near, 0)

    @pl.when(c >= far)
    def _():
        far_stats()

    for h in range(GROUP):
        inverse = 1.0 / total[h]
        total[h] = inverse
        weighted[h] = weighted[h] * inverse

    def tile_grads(d):
        sides = []
        for h in range(GROUP):
            p = ws[h, d].astype(F32) * (jnp.exp2(tops[d, h] - top[h]) * total[h])
            ds = (p * (gps[d, h] - weighted[h])).astype(BF16)
            sides.append((ds, p.astype(BF16)))
            if h % 2 == 1:
                both = pl.ds(h - 1, 2)
                key_part = dot_nn(jnp.concatenate([one[0] for one in sides], axis=1), qs[both].reshape(2 * ROWS, HEAD_DIM))
                value_part = dot_nn(jnp.concatenate([one[1] for one in sides], axis=1), gs[both].reshape(2 * ROWS, HEAD_DIM))
                sides = []
                if h == 1:
                    acc[0] = key_part
                    acc[1] = value_part
                else:
                    acc[0] += key_part
                    acc[1] += value_part
            ws[h, d] = ds

    def far_grads():
        far_kt[...] = jnp.transpose(kv[far, 0, BLK:].astype(F32)).astype(BF16)
        acc[...] = jnp.zeros_like(acc)
        for h in range(GROUP):
            p = far_ws[h].astype(F32) * (jnp.exp2(tops[far, h, :, :BLK] - top[h, :, :BLK]) * total[h, :, :BLK])
            ds = (p * (far_gps[h] - weighted[h, :, :BLK])).astype(BF16)
            acc[0, BLK:] += dot_nn(ds, qs[h, :BLK])
            acc[1, BLK:] += dot_nn(p.astype(BF16), gs[h, :BLK])
            dqt[h, :, :BLK] = dot_nn(far_kt[...], ds)

    def pair_copy(d):
        slot = (d + 1 - 2 * core) // 2
        return remote(stage.at[d], pair.at[slot], pair_send.at[d // 2], pair_recv.at[slot], ctx=sibling)

    def pair_wait(m):
        remote(stage.at[0], pair.at[m], pair_send.at[0], pair_recv.at[m], ctx=sibling).wait_recv()

    def back_copy(m):
        return remote(stage.at[2 * m], back.at[m], back_send.at[m], back_recv.at[m], ctx=(c + size - 2 * m) % size)

    def inward(step, carry):
        m = FAR - step // 2
        d = 2 * m - 1 + step % 2

        @pl.when((d < far) & (c >= d))
        def _():
            tile_grads(d)

        @pl.when((d == far) & (c >= d))
        def _():
            far_grads()

        @pl.when((step % 2 == 0) & (c >= d))
        def _():
            stage[d] = acc[...].astype(BF16)
            pair_copy(d).start()

        @pl.when((step % 2 == 1) & (c >= d))
        def _():
            @pl.when((m < FAR) | (core == 1))
            def _():
                pair_wait(m)
                acc[...] += pair[m].astype(F32)

            stage[d] = acc[...].astype(BF16)
            back_copy(m).start()

        return carry

    lax.fori_loop(0, far, inward, 0)
    tile_grads(0)

    for h in range(GROUP):
        gradient = dqt[h] + dot_nn(kt[...], ws[h].reshape(far * ROWS, ROWS))
        a_ref[:, h * HEAD_DIM:(h + 1) * HEAD_DIM] = rope_back(jnp.transpose(gradient) * SCALE).astype(BF16)

    @pl.when(core == 0)
    def _():
        pair_wait(0)
        acc[...] += pair[0].astype(F32)

    for m in range(FAR, 0, -1):
        @pl.when(chip + m < chips)
        def _():
            back_copy(m).wait_recv()
            acc[...] += back[m].astype(F32)

    a_ref[:, base:base + HEAD_DIM] = rope_back(acc[0] * SCALE).astype(BF16)
    a_ref[:, base + HEAD_DIM:DEPTH] = acc[1].astype(BF16)

    kept_half = (((z + 1) // 2) % 2, z // 2)
    kept_part = (z // 2, z % 2)

    def order(i, kind):
        x_first = i == X_STEP
        half = kept_half[kind]
        return (
            jnp.where(x_first, x, half),
            jnp.where(x_first, half, x),
            jnp.where(x_first, across, z_pairs[kind]),
            jnp.where(x_first, z_pairs[kind], across),
        )

    def first_copy(i, kind):
        n = 2 * i + kind
        kept, _, partner, _ = order(i, kind)
        return remote(s1.at[n, 1 - kept], r1.at[n], s1_send.at[n], s1_recv.at[n], tp=partner)

    def second_copy(i, kind):
        n = 2 * i + kind
        _, kept, _, partner = order(i, kind)
        return remote(s2.at[n, 1 - kept], r2.at[n], s2_send.at[n], s2_recv.at[n], tp=partner)

    def third_copy(i, kind):
        n = 2 * i + kind
        return remote(s3.at[n, 1 - kept_part[kind]], r3.at[n], s3_send.at[n], s3_recv.at[n], tp=z_pairs[1 - kind])

    def compute(i):
        @pl.when(i + RING - 1 < STEPS)
        def _():
            for load in loads(i + RING - 1):
                load.start()

        for load in loads(i):
            load.wait()
        for kind in range(2):
            n = 2 * i + kind
            product = dot_nt(a_ref[...], w[i % RING, kind * WIDE:(kind + 1) * WIDE, :]).astype(BF16)
            for to_z in range(4):
                half = ((to_z + 1) // 2 % 2, to_z // 2)[kind]
                part = (to_z // 2, to_z % 2)[kind]
                for to_x in range(2):
                    rows = to_z * 64 + to_x * 32
                    outer = jnp.where(i == X_STEP, to_x, half)
                    inner = jnp.where(i == X_STEP, half, to_x)
                    to = pl.multiple_of(inner * 64 + part * 32, 32)
                    s1[n, outer, pl.ds(to, 32)] = product[rows:rows + 32]
            first_copy(i, kind).start()

    def second(i):
        for kind in range(2):
            n = 2 * i + kind
            first_copy(i, kind).wait_recv()
            value = (s1[n, order(i, kind)[0]].astype(F32) + r1[n].astype(F32)).astype(BF16)
            s2[n, 0] = value[:64]
            s2[n, 1] = value[64:]
            second_copy(i, kind).start()

    def third(i):
        for kind in range(2):
            n = 2 * i + kind
            second_copy(i, kind).wait_recv()
            value = (s2[n, order(i, kind)[1]].astype(F32) + r2[n].astype(F32)).astype(BF16)
            s3[n, 0] = value[:32]
            s3[n, 1] = value[32:]
            third_copy(i, kind).start()

    def last(i):
        for kind in range(2):
            n = 2 * i + kind
            third_copy(i, kind).wait_recv()
            value = s3[n, kept_part[kind]].astype(F32) + r3[n].astype(F32)
            out_ref[:, pl.ds(i * WIDTH + kind * WIDE, WIDE)] = value.astype(BF16)

    def step(i, carry):
        @pl.when(i < STEPS)
        def _():
            compute(i)

        for number, work in enumerate((second, third, last)):
            lag = (number + 1) * LAG

            @pl.when((i >= lag) & (i < STEPS + lag))
            def _():
                work(i - lag)

        return carry

    lax.fori_loop(0, STEPS + 3 * LAG, step, 0)

    def drain(i, carry):
        for kind in range(2):
            first_copy(i, kind).wait_send()
            second_copy(i, kind).wait_send()
            third_copy(i, kind).wait_send()
        return carry

    lax.fori_loop(0, STEPS, drain, 0)

    for m in range(FAR + 1):
        @pl.when(passes(m))
        def _():
            pass_copy(m).wait_send()

    for m in range(1, FAR + 1):
        @pl.when(chip + m < chips)
        def _():
            key_copy(m).wait_send()

        @pl.when(c >= 2 * m - 1)
        def _():
            pair_copy(2 * m - 1).wait_send()

        @pl.when(chip >= m)
        def _():
            back_copy(m).wait_send()


def layer(q, k, v, g, docs, wq, wk, wv):
    any_spec = pl.BlockSpec(memory_space=pl.ANY)
    slots = 2 * FAR + 1
    dma = pltpu.SemaphoreType.DMA
    width = wq.shape[0]
    chunks = 2 * STEPS
    return pl.pallas_call(
        layer_kernel,
        out_shape=pltpu.VMEM((ROWS // 8, width), BF16),
        in_specs=[any_spec] * 4 + [pl.BlockSpec(memory_space=pltpu.SMEM)] + [any_spec] * 3,
        out_specs=pl.BlockSpec(memory_space=pltpu.VMEM),
        scratch_shapes=[
            pltpu.VMEM((slots, 2, ROWS, HEAD_DIM), BF16),
            pltpu.VMEM((GROUP, ROWS, HEAD_DIM), BF16),
            pltpu.VMEM((GROUP, ROWS, HEAD_DIM), BF16),
            pltpu.VMEM((GROUP, slots - 1, ROWS, ROWS), BF16),
            pltpu.VMEM((slots - 1, GROUP, ROWS, ROWS), F32),
            pltpu.VMEM((GROUP, BLK, BLK), BF16),
            pltpu.VMEM((GROUP, BLK, BLK), F32),
            pltpu.VMEM((slots, GROUP, 1, ROWS), F32),
            pltpu.VMEM((GROUP, 1, ROWS), F32),
            pltpu.VMEM((GROUP, 1, ROWS), F32),
            pltpu.VMEM((GROUP, 1, ROWS), F32),
            pltpu.VMEM((GROUP, HEAD_DIM, ROWS), F32),
            pltpu.VMEM((HEAD_DIM, (slots - 1) * ROWS), BF16),
            pltpu.VMEM((HEAD_DIM, BLK), BF16),
            pltpu.VMEM((2, ROWS, HEAD_DIM), F32),
            pltpu.VMEM((slots, 2, ROWS, HEAD_DIM), BF16),
            pltpu.VMEM((FAR + 1, 2, ROWS, HEAD_DIM), BF16),
            pltpu.VMEM((FAR + 1, 2, ROWS, HEAD_DIM), BF16),
            pltpu.VMEM((ROWS, HEAD_DIM), F32),
            pltpu.VMEM((ROWS, HEAD_DIM), F32),
            pltpu.VMEM((ROWS, DEPTH), BF16),
            pltpu.VMEM((RING, WIDTH, DEPTH), BF16),
            pltpu.VMEM((chunks, 2, 128, WIDE), BF16),
            pltpu.VMEM((chunks, 128, WIDE), BF16),
            pltpu.VMEM((chunks, 2, 64, WIDE), BF16),
            pltpu.VMEM((chunks, 64, WIDE), BF16),
            pltpu.VMEM((chunks, 2, 32, WIDE), BF16),
            pltpu.VMEM((chunks, 32, WIDE), BF16),
            dma((GROUP,)),
            dma((GROUP,)),
            dma((2,)),
            dma((FAR + 1,)),
            dma((slots,)),
            dma((FAR + 1,)),
            dma((FAR + 1,)),
            dma((FAR + 1,)),
            dma((FAR + 1,)),
            dma((FAR + 1,)),
            dma((RING, 3)),
        ] + [dma((chunks,))] * 6,
        compiler_params=pltpu.CompilerParams(
            collective_id=0, has_side_effects=True, vmem_limit_bytes=60 * 1024 * 1024
        ),
        name="layer",
    )(q, k, v, g, docs, wq, wk, wv)


def local(query_rows, key_rows, value_rows, grad_out, doc_ids, w_query, w_key, w_value):
    return layer(query_rows, key_rows, value_rows, grad_out, doc_ids, w_query, w_key, w_value)


def solution(mesh):
    in_specs = (
        P("ctx", "tp"),
        P("ctx", "tp"),
        P("ctx", "tp"),
        P("ctx", "tp"),
        P(),
        P(None, "tp"),
        P(None, "tp"),
        P(None, "tp"),
    )
    out_specs = P(("ctx", "tp"), None)
    return jax.shard_map(local, mesh=mesh, in_specs=in_specs, out_specs=out_specs, check_vma=False)
```

```python
import functools
import math

import jax
import jax.numpy as jnp
from jax import lax
from jax.experimental import pallas as pl
from jax.experimental.pallas import tpu as pltpu
from jax.sharding import PartitionSpec as P

HEADS = 64
KV_HEADS = 8
HEAD_DIM = 128
BLK = 128
GROUP = HEADS // KV_HEADS
BLOCKS = 32
THETA = 500000.0
NEGATIVE = -1e30
ROWS = 256
FAR = 4
SCALE = HEAD_DIM ** (-0.5)
LOG2_SCALE = SCALE * math.log2(math.e)
STEPS = 8
WIDTH = 1024
WIDE = WIDTH // 2
RING = 3
LAG = 3
X_STEP = 1
DEPTH = GROUP * HEAD_DIM + 2 * HEAD_DIM
F32 = jnp.float32
BF16 = jnp.bfloat16


def dot_nt(left, right):
    return lax.dot_general(left, right, (((1,), (1,)), ((), ())), preferred_element_type=F32)


def dot_nn(left, right):
    return lax.dot_general(left, right, (((1,), (0,)), ((), ())), preferred_element_type=F32)


def remote(src, dst, send, recv, **device):
    return pltpu.make_async_remote_copy(
        src_ref=src, dst_ref=dst, send_sem=send, recv_sem=recv,
        device_id=device, device_id_type=pl.DeviceIdType.MESH,
    )


def layer_kernel(
    q_hbm, k_hbm, v_hbm, g_hbm, docs, wq, wk, wv, out_ref,
    kv, qs, gs, ws, gps, far_ws, far_gps, tops, top, total, weighted, dqt, kt, far_kt, acc, stage, pair, back, cosine, sine,
    a_ref, early, w, s1, r1, s2, r2, s3, r3,
    q_sem, g_sem, own_sem, kv_send, kv_recv, pass_send, pair_send, pair_recv, back_send, back_recv,
    w_sem, s1_send, s1_recv, s2_send, s2_recv, s3_send, s3_recv,
):
    c = lax.axis_index("ctx")
    size = lax.axis_size("ctx")
    chips = size // 2
    chip, core = c // 2, c % 2
    sibling = c + 1 - 2 * core

    t = lax.axis_index("tp")
    z, x = t // 2, t % 2
    across = t + 1 - 2 * x
    z_pairs = (2 * (z + 1 - 2 * (z % 2)) + x, 2 * (3 - z) + x)

    barrier = pltpu.get_barrier_semaphore()
    pl.semaphore_signal(barrier, inc=1, device_id={"ctx": sibling}, device_id_type=pl.DeviceIdType.MESH)
    for m in range(1, chips):
        pl.semaphore_signal(barrier, inc=1, device_id={"ctx": (c + 2 * m) % size}, device_id_type=pl.DeviceIdType.MESH)
    for other in (across,) + z_pairs:
        pl.semaphore_signal(barrier, inc=1, device_id={"tp": other}, device_id_type=pl.DeviceIdType.MESH)
    q_loads = [pltpu.make_async_copy(q_hbm.at[:, pl.ds(h * HEAD_DIM, HEAD_DIM)], qs.at[h], q_sem.at[h]) for h in range(GROUP)]
    g_loads = [pltpu.make_async_copy(g_hbm.at[:, pl.ds(h * HEAD_DIM, HEAD_DIM)], gs.at[h], g_sem.at[h]) for h in range(GROUP)]
    own_loads = [pltpu.make_async_copy(k_hbm, kv.at[0, 0], own_sem.at[0]), pltpu.make_async_copy(v_hbm, kv.at[0, 1], own_sem.at[1])]
    for load in own_loads + q_loads + g_loads:
        load.start()

    base = GROUP * HEAD_DIM

    def loads(i):
        rows = pl.ds(i * WIDTH, WIDTH)
        slot = i % RING
        return [
            pltpu.make_async_copy(wq.at[rows], w.at[slot, :, 0:base], w_sem.at[slot, 0]),
            pltpu.make_async_copy(wk.at[rows], w.at[slot, :, base:base + HEAD_DIM], w_sem.at[slot, 1]),
            pltpu.make_async_copy(wv.at[rows], w.at[slot, :, base + HEAD_DIM:DEPTH], w_sem.at[slot, 2]),
        ]

    pl.semaphore_wait(barrier, chips + 3)

    for load in own_loads:
        load.wait()

    def key_copy(m):
        return remote(kv.at[0], kv.at[2 * m], kv_send.at[m], kv_recv.at[2 * m], ctx=(c + 2 * m) % size)

    def pass_copy(m):
        slot = 2 * m + 1 - 2 * core
        return remote(kv.at[2 * m], kv.at[slot], pass_send.at[m], kv_recv.at[slot], ctx=sibling)

    def passes(m):
        return (chip >= m) & ((m > 0) | (core == 0)) & ((m < FAR) | (core == 1))

    @pl.when(core == 0)
    def _():
        pass_copy(0).start()

    for m in range(1, FAR + 1):
        @pl.when(chip + m < chips)
        def _():
            key_copy(m).start()

    starts = []
    for block in range(2):
        document = docs[2 * c + block]
        starts.append(sum([(docs[b] < document).astype(jnp.int32) for b in range(BLOCKS)]))
    lane = lax.broadcasted_iota(jnp.int32, (1, ROWS), 1)
    start_row = jnp.where(lane < BLK, starts[0], starts[1])

    dqt[...] = jnp.zeros_like(dqt)
    for load in q_loads + g_loads:
        load.wait()

    key_at = lax.broadcasted_iota(jnp.int32, (ROWS, ROWS), 0)
    query_at = lax.broadcasted_iota(jnp.int32, (ROWS, ROWS), 1)
    far = 2 * FAR

    def shifted_exp(s, row, bias):
        return jnp.concatenate(
            [jnp.exp2(s[b * BLK:(b + 1) * BLK] * LOG2_SCALE - (row - bias[b])) for b in range(2)], axis=0
        )

    def tile_stats(d, first):
        key_block = 2 * (c - d)
        bias = [jnp.where(key_block + b >= start_row, 0.0, NEGATIVE) for b in range(2)]
        for h in range(GROUP):
            s = dot_nt(kv[d, 0], qs[h])
            gp = dot_nt(kv[d, 1], gs[h])
            gps[d, h] = gp
            if first:
                s = jnp.where(key_at <= query_at, s, NEGATIVE)
            new = jnp.maximum(*[
                jnp.max(s[b * BLK:(b + 1) * BLK], axis=0, keepdims=True) * LOG2_SCALE + bias[b] for b in range(2)
            ])
            if not first:
                old = top[h]
                new = jnp.maximum(old, new)
            halves = [jnp.exp2(s[b * BLK:(b + 1) * BLK] * LOG2_SCALE - (new - bias[b])) for b in range(2)]
            part = jnp.sum(halves[0] + halves[1], axis=0, keepdims=True)
            part_weighted = jnp.sum(halves[0] * gp[:BLK] + halves[1] * gp[BLK:], axis=0, keepdims=True)
            if not first:
                factor = jnp.exp2(old - new)
                part = total[h] * factor + part
                part_weighted = weighted[h] * factor + part_weighted
            top[h] = new
            tops[d, h] = new
            total[h] = part
            weighted[h] = part_weighted
            for b in range(2):
                ws[h, d, b * BLK:(b + 1) * BLK] = halves[b].astype(BF16)

    def far_stats():
        bias = jnp.where(2 * (c - far) + 1 >= starts[0], 0.0, NEGATIVE)
        for h in range(GROUP):
            s = dot_nt(kv[far, 0, BLK:], qs[h, :BLK])
            gp = dot_nt(kv[far, 1, BLK:], gs[h, :BLK])
            old = top[h, :, :BLK]
            new = jnp.maximum(old, jnp.max(s, axis=0, keepdims=True) * LOG2_SCALE + bias)
            w = jnp.exp2(s * LOG2_SCALE - (new - bias))
            factor = jnp.exp2(old - new)
            top[h, :, :BLK] = new
            tops[far, h, :, :BLK] = new
            total[h, :, :BLK] = total[h, :, :BLK] * factor + jnp.sum(w, axis=0, keepdims=True)
            weighted[h, :, :BLK] = weighted[h, :, :BLK] * factor + jnp.sum(w * gp, axis=0, keepdims=True)
            far_ws[h] = w.astype(BF16)
            far_gps[h] = gp

    tile_stats(0, True)

    for i in range(RING - 1):
        for load in loads(i):
            load.start()
    kt[:, :ROWS] = jnp.transpose(kv[0, 0].astype(F32)).astype(BF16)

    def near(d, carry):
        m = (d + 1) // 2

        @pl.when((d % 2 == 1) & (chip >= m))
        def _():
            key_copy(m).wait_recv()

            @pl.when(passes(m))
            def _():
                pass_copy(m).start()

        @pl.when(c >= d)
        def _():
            @pl.when(d % 2 == 1)
            def _():
                remote(kv.at[d], kv.at[d], pass_send.at[0], kv_recv.at[d], ctx=sibling).wait_recv()

            tile_stats(d, False)
            kt[:, pl.ds(pl.multiple_of(d * ROWS, ROWS), ROWS)] = jnp.transpose(kv[d, 0].astype(F32)).astype(BF16)

        @pl.when(c < d)
        def _():
            kt[:, pl.ds(pl.multiple_of(d * ROWS, ROWS), ROWS)] = jnp.zeros((HEAD_DIM, ROWS), BF16)
            for h in range(GROUP):
                ws[h, d] = jnp.zeros((ROWS, ROWS), BF16)

        return carry

    lax.fori_loop(1, far, near, 0)

    @pl.when(c >= far)
    def _():
        far_stats()

    for h in range(GROUP):
        inverse = 1.0 / total[h]
        total[h] = inverse
        weighted[h] = weighted[h] * inverse

    def tile_grads(d):
        sides = []
        for h in range(GROUP):
            p = ws[h, d].astype(F32) * (jnp.exp2(tops[d, h] - top[h]) * total[h])
            ds = (p * (gps[d, h] - weighted[h])).astype(BF16)
            sides.append((ds, p.astype(BF16)))
            if h % 2 == 1:
                both = pl.ds(h - 1, 2)
                key_part = dot_nn(jnp.concatenate([one[0] for one in sides], axis=1), qs[both].reshape(2 * ROWS, HEAD_DIM))
                value_part = dot_nn(jnp.concatenate([one[1] for one in sides], axis=1), gs[both].reshape(2 * ROWS, HEAD_DIM))
                sides = []
                if h == 1:
                    acc[0] = key_part
                    acc[1] = value_part
                else:
                    acc[0] += key_part
                    acc[1] += value_part
            ws[h, d] = ds

    def far_grads():
        far_kt[...] = jnp.transpose(kv[far, 0, BLK:].astype(F32)).astype(BF16)
        acc[...] = jnp.zeros_like(acc)
        for h in range(GROUP):
            p = far_ws[h].astype(F32) * (jnp.exp2(tops[far, h, :, :BLK] - top[h, :, :BLK]) * total[h, :, :BLK])
            ds = (p * (far_gps[h] - weighted[h, :, :BLK])).astype(BF16)
            acc[0, BLK:] += dot_nn(ds, qs[h, :BLK])
            acc[1, BLK:] += dot_nn(p.astype(BF16), gs[h, :BLK])
            dqt[h, :, :BLK] = dot_nn(far_kt[...], ds)

    def pair_copy(d):
        slot = (d + 1 - 2 * core) // 2
        return remote(stage.at[d], pair.at[slot], pair_send.at[d // 2], pair_recv.at[slot], ctx=sibling)

    def pair_wait(m):
        remote(stage.at[0], pair.at[m], pair_send.at[0], pair_recv.at[m], ctx=sibling).wait_recv()

    def back_copy(m):
        return remote(stage.at[2 * m], back.at[m], back_send.at[m], back_recv.at[m], ctx=(c + size - 2 * m) % size)

    def inward(step, carry):
        m = FAR - step // 2
        d = 2 * m - 1 + step % 2

        @pl.when((d < far) & (c >= d))
        def _():
            tile_grads(d)

        @pl.when((d == far) & (c >= d))
        def _():
            far_grads()

        @pl.when((step % 2 == 0) & (c >= d))
        def _():
            stage[d] = acc[...].astype(BF16)
            pair_copy(d).start()

        @pl.when((step % 2 == 1) & (c >= d))
        def _():
            @pl.when((m < FAR) | (core == 1))
            def _():
                pair_wait(m)
                acc[...] += pair[m].astype(F32)

            stage[d] = acc[...].astype(BF16)
            back_copy(m).start()

        return carry

    lax.fori_loop(0, far, inward, 0)
    tile_grads(0)

    places = (c * ROWS + lax.broadcasted_iota(jnp.int32, (ROWS, HEAD_DIM), 0)).astype(F32)
    lanes = lax.broadcasted_iota(jnp.int32, (ROWS, HEAD_DIM), 1)
    half = HEAD_DIM // 2
    pair_lane = jnp.where(lanes < half, lanes, lanes - half).astype(F32)
    angles = places * jnp.exp(pair_lane * (-2.0 * math.log(THETA) / HEAD_DIM))
    cosine[...] = jnp.cos(angles)
    sine[...] = jnp.where(lanes < half, 1.0, -1.0) * jnp.sin(angles)

    def rope_back(y):
        return y * cosine[...] + pltpu.roll(y, half, 1) * sine[...]

    for h in range(GROUP):
        gradient = dqt[h] + dot_nn(kt[...], ws[h].reshape(far * ROWS, ROWS))
        a_ref[:, h * HEAD_DIM:(h + 1) * HEAD_DIM] = rope_back(jnp.transpose(gradient) * SCALE).astype(BF16)

    for load in loads(0):
        load.wait()
    for kind in range(2):
        early[kind] = dot_nt(a_ref[:, :base], w[0, kind * WIDE:(kind + 1) * WIDE, :base])

    @pl.when(core == 0)
    def _():
        pair_wait(0)
        acc[...] += pair[0].astype(F32)

    for m in range(FAR, 0, -1):
        @pl.when(chip + m < chips)
        def _():
            back_copy(m).wait_recv()
            acc[...] += back[m].astype(F32)

    a_ref[:, base:base + HEAD_DIM] = rope_back(acc[0] * SCALE).astype(BF16)
    a_ref[:, base + HEAD_DIM:DEPTH] = acc[1].astype(BF16)

    kept_half = (((z + 1) // 2) % 2, z // 2)
    kept_part = (z // 2, z % 2)

    def order(i, kind):
        x_first = i == X_STEP
        half = kept_half[kind]
        return (
            jnp.where(x_first, x, half),
            jnp.where(x_first, half, x),
            jnp.where(x_first, across, z_pairs[kind]),
            jnp.where(x_first, z_pairs[kind], across),
        )

    def first_copy(i, kind):
        n = 2 * i + kind
        kept, _, partner, _ = order(i, kind)
        return remote(s1.at[n, 1 - kept], r1.at[n], s1_send.at[n], s1_recv.at[n], tp=partner)

    def second_copy(i, kind):
        n = 2 * i + kind
        _, kept, _, partner = order(i, kind)
        return remote(s2.at[n, 1 - kept], r2.at[n], s2_send.at[n], s2_recv.at[n], tp=partner)

    def third_copy(i, kind):
        n = 2 * i + kind
        return remote(s3.at[n, 1 - kept_part[kind]], r3.at[n], s3_send.at[n], s3_recv.at[n], tp=z_pairs[1 - kind])

    def compute(i):
        @pl.when(i + RING - 1 < STEPS)
        def _():
            for load in loads(i + RING - 1):
                load.start()

        @pl.when(i > 0)
        def _():
            for load in loads(i):
                load.wait()

        for kind in range(2):
            n = 2 * i + kind
            @pl.when(i == 0)
            def _():
                early[kind] += dot_nt(a_ref[:, base:], w[0, kind * WIDE:(kind + 1) * WIDE, base:])

            @pl.when(i > 0)
            def _():
                early[kind] = dot_nt(a_ref[...], w[i % RING, kind * WIDE:(kind + 1) * WIDE, :])

            product = early[kind].astype(BF16)
            for to_z in range(4):
                half = ((to_z + 1) // 2 % 2, to_z // 2)[kind]
                part = (to_z // 2, to_z % 2)[kind]
                for to_x in range(2):
                    rows = to_z * 64 + to_x * 32
                    outer = jnp.where(i == X_STEP, to_x, half)
                    inner = jnp.where(i == X_STEP, half, to_x)
                    to = pl.multiple_of(inner * 64 + part * 32, 32)
                    s1[n, outer, pl.ds(to, 32)] = product[rows:rows + 32]
            first_copy(i, kind).start()

    def second(i):
        for kind in range(2):
            n = 2 * i + kind
            first_copy(i, kind).wait_recv()
            value = (s1[n, order(i, kind)[0]].astype(F32) + r1[n].astype(F32)).astype(BF16)
            s2[n, 0] = value[:64]
            s2[n, 1] = value[64:]
            second_copy(i, kind).start()

    def third(i):
        for kind in range(2):
            n = 2 * i + kind
            second_copy(i, kind).wait_recv()
            value = (s2[n, order(i, kind)[1]].astype(F32) + r2[n].astype(F32)).astype(BF16)
            s3[n, 0] = value[:32]
            s3[n, 1] = value[32:]
            third_copy(i, kind).start()

    def last(i):
        for kind in range(2):
            n = 2 * i + kind
            third_copy(i, kind).wait_recv()
            value = s3[n, kept_part[kind]].astype(F32) + r3[n].astype(F32)
            out_ref[:, pl.ds(i * WIDTH + kind * WIDE, WIDE)] = value.astype(BF16)

    def step(i, carry):
        @pl.when(i < STEPS)
        def _():
            compute(i)

        for number, work in enumerate((second, third, last)):
            lag = (number + 1) * LAG

            @pl.when((i >= lag) & (i < STEPS + lag))
            def _():
                work(i - lag)

        return carry

    lax.fori_loop(0, STEPS + 3 * LAG, step, 0)

    def drain(i, carry):
        for kind in range(2):
            first_copy(i, kind).wait_send()
            second_copy(i, kind).wait_send()
            third_copy(i, kind).wait_send()
        return carry

    lax.fori_loop(0, STEPS, drain, 0)

    for m in range(FAR + 1):
        @pl.when(passes(m))
        def _():
            pass_copy(m).wait_send()

    for m in range(1, FAR + 1):
        @pl.when(chip + m < chips)
        def _():
            key_copy(m).wait_send()

        @pl.when(c >= 2 * m - 1)
        def _():
            pair_copy(2 * m - 1).wait_send()

        @pl.when(chip >= m)
        def _():
            back_copy(m).wait_send()


def layer(q, k, v, g, docs, wq, wk, wv):
    any_spec = pl.BlockSpec(memory_space=pl.ANY)
    slots = 2 * FAR + 1
    dma = pltpu.SemaphoreType.DMA
    width = wq.shape[0]
    chunks = 2 * STEPS
    return pl.pallas_call(
        layer_kernel,
        out_shape=pltpu.VMEM((ROWS // 8, width), BF16),
        in_specs=[any_spec] * 4 + [pl.BlockSpec(memory_space=pltpu.SMEM)] + [any_spec] * 3,
        out_specs=pl.BlockSpec(memory_space=pltpu.VMEM),
        scratch_shapes=[
            pltpu.VMEM((slots, 2, ROWS, HEAD_DIM), BF16),
            pltpu.VMEM((GROUP, ROWS, HEAD_DIM), BF16),
            pltpu.VMEM((GROUP, ROWS, HEAD_DIM), BF16),
            pltpu.VMEM((GROUP, slots - 1, ROWS, ROWS), BF16),
            pltpu.VMEM((slots - 1, GROUP, ROWS, ROWS), F32),
            pltpu.VMEM((GROUP, BLK, BLK), BF16),
            pltpu.VMEM((GROUP, BLK, BLK), F32),
            pltpu.VMEM((slots, GROUP, 1, ROWS), F32),
            pltpu.VMEM((GROUP, 1, ROWS), F32),
            pltpu.VMEM((GROUP, 1, ROWS), F32),
            pltpu.VMEM((GROUP, 1, ROWS), F32),
            pltpu.VMEM((GROUP, HEAD_DIM, ROWS), F32),
            pltpu.VMEM((HEAD_DIM, (slots - 1) * ROWS), BF16),
            pltpu.VMEM((HEAD_DIM, BLK), BF16),
            pltpu.VMEM((2, ROWS, HEAD_DIM), F32),
            pltpu.VMEM((slots, 2, ROWS, HEAD_DIM), BF16),
            pltpu.VMEM((FAR + 1, 2, ROWS, HEAD_DIM), BF16),
            pltpu.VMEM((FAR + 1, 2, ROWS, HEAD_DIM), BF16),
            pltpu.VMEM((ROWS, HEAD_DIM), F32),
            pltpu.VMEM((ROWS, HEAD_DIM), F32),
            pltpu.VMEM((ROWS, DEPTH), BF16),
            pltpu.VMEM((2, ROWS, WIDE), F32),
            pltpu.VMEM((RING, WIDTH, DEPTH), BF16),
            pltpu.VMEM((chunks, 2, 128, WIDE), BF16),
            pltpu.VMEM((chunks, 128, WIDE), BF16),
            pltpu.VMEM((chunks, 2, 64, WIDE), BF16),
            pltpu.VMEM((chunks, 64, WIDE), BF16),
            pltpu.VMEM((chunks, 2, 32, WIDE), BF16),
            pltpu.VMEM((chunks, 32, WIDE), BF16),
            dma((GROUP,)),
            dma((GROUP,)),
            dma((2,)),
            dma((FAR + 1,)),
            dma((slots,)),
            dma((FAR + 1,)),
            dma((FAR + 1,)),
            dma((FAR + 1,)),
            dma((FAR + 1,)),
            dma((FAR + 1,)),
            dma((RING, 3)),
        ] + [dma((chunks,))] * 6,
        compiler_params=pltpu.CompilerParams(
            collective_id=0, has_side_effects=True, vmem_limit_bytes=60 * 1024 * 1024
        ),
        name="layer",
    )(q, k, v, g, docs, wq, wk, wv)


def local(query_rows, key_rows, value_rows, grad_out, doc_ids, w_query, w_key, w_value):
    return layer(query_rows, key_rows, value_rows, grad_out, doc_ids, w_query, w_key, w_value)


def solution(mesh):
    in_specs = (
        P("ctx", "tp"),
        P("ctx", "tp"),
        P("ctx", "tp"),
        P("ctx", "tp"),
        P(),
        P(None, "tp"),
        P(None, "tp"),
        P(None, "tp"),
    )
    out_specs = P(("ctx", "tp"), None)
    return jax.shard_map(local, mesh=mesh, in_specs=in_specs, out_specs=out_specs, check_vma=False)
```

```python
import functools
import math

import jax
import jax.numpy as jnp
from jax import lax
from jax.experimental import pallas as pl
from jax.experimental.pallas import tpu as pltpu
from jax.sharding import PartitionSpec as P

HEADS = 64
KV_HEADS = 8
HEAD_DIM = 128
BLK = 128
GROUP = HEADS // KV_HEADS
BLOCKS = 32
THETA = 500000.0
NEGATIVE = -1e30
ROWS = 256
FAR = 4
SCALE = HEAD_DIM ** (-0.5)
LOG2_SCALE = SCALE * math.log2(math.e)
STEPS = 8
WIDTH = 1024
WIDE = WIDTH // 2
RING = 3
LAG = 3
EARLY = 2
X_STEP = 1
DEPTH = GROUP * HEAD_DIM + 2 * HEAD_DIM
F32 = jnp.float32
BF16 = jnp.bfloat16


def dot_nt(left, right):
    return lax.dot_general(left, right, (((1,), (1,)), ((), ())), preferred_element_type=F32)


def dot_nn(left, right):
    return lax.dot_general(left, right, (((1,), (0,)), ((), ())), preferred_element_type=F32)


def remote(src, dst, send, recv, **device):
    return pltpu.make_async_remote_copy(
        src_ref=src, dst_ref=dst, send_sem=send, recv_sem=recv,
        device_id=device, device_id_type=pl.DeviceIdType.MESH,
    )


def layer_kernel(
    q_hbm, k_hbm, v_hbm, g_hbm, docs, wq, wk, wv, out_ref,
    kv, qs, gs, ws, gps, far_ws, far_gps, tops, top, total, weighted, dqt, kt, far_kt, acc, stage, pair, back, cosine, sine,
    a_ref, early, w, s1, r1, s2, r2, s3, r3,
    q_sem, g_sem, own_sem, kv_send, kv_recv, pass_send, pair_send, pair_recv, back_send, back_recv,
    w_sem, s1_send, s1_recv, s2_send, s2_recv, s3_send, s3_recv,
):
    c = lax.axis_index("ctx")
    size = lax.axis_size("ctx")
    chips = size // 2
    chip, core = c // 2, c % 2
    sibling = c + 1 - 2 * core

    t = lax.axis_index("tp")
    z, x = t // 2, t % 2
    across = t + 1 - 2 * x
    z_pairs = (2 * (z + 1 - 2 * (z % 2)) + x, 2 * (3 - z) + x)

    barrier = pltpu.get_barrier_semaphore()
    pl.semaphore_signal(barrier, inc=1, device_id={"ctx": sibling}, device_id_type=pl.DeviceIdType.MESH)
    for m in range(1, chips):
        pl.semaphore_signal(barrier, inc=1, device_id={"ctx": (c + 2 * m) % size}, device_id_type=pl.DeviceIdType.MESH)
    for other in (across,) + z_pairs:
        pl.semaphore_signal(barrier, inc=1, device_id={"tp": other}, device_id_type=pl.DeviceIdType.MESH)
    q_loads = [pltpu.make_async_copy(q_hbm.at[:, pl.ds(h * HEAD_DIM, HEAD_DIM)], qs.at[h], q_sem.at[h]) for h in range(GROUP)]
    g_loads = [pltpu.make_async_copy(g_hbm.at[:, pl.ds(h * HEAD_DIM, HEAD_DIM)], gs.at[h], g_sem.at[h]) for h in range(GROUP)]
    own_loads = [pltpu.make_async_copy(k_hbm, kv.at[0, 0], own_sem.at[0]), pltpu.make_async_copy(v_hbm, kv.at[0, 1], own_sem.at[1])]
    for load in own_loads + q_loads + g_loads:
        load.start()

    base = GROUP * HEAD_DIM

    def loads(i):
        rows = pl.ds(i * WIDTH, WIDTH)
        slot = i % RING
        return [
            pltpu.make_async_copy(wq.at[rows], w.at[slot, :, 0:base], w_sem.at[slot, 0]),
            pltpu.make_async_copy(wk.at[rows], w.at[slot, :, base:base + HEAD_DIM], w_sem.at[slot, 1]),
            pltpu.make_async_copy(wv.at[rows], w.at[slot, :, base + HEAD_DIM:DEPTH], w_sem.at[slot, 2]),
        ]

    pl.semaphore_wait(barrier, chips + 3)

    for load in own_loads:
        load.wait()

    def key_copy(m):
        return remote(kv.at[0], kv.at[2 * m], kv_send.at[m], kv_recv.at[2 * m], ctx=(c + 2 * m) % size)

    def pass_copy(m):
        slot = 2 * m + 1 - 2 * core
        return remote(kv.at[2 * m], kv.at[slot], pass_send.at[m], kv_recv.at[slot], ctx=sibling)

    def passes(m):
        return (chip >= m) & ((m > 0) | (core == 0)) & ((m < FAR) | (core == 1))

    @pl.when(core == 0)
    def _():
        pass_copy(0).start()

    for m in range(1, FAR + 1):
        @pl.when(chip + m < chips)
        def _():
            key_copy(m).start()

    starts = []
    for block in range(2):
        document = docs[2 * c + block]
        starts.append(sum([(docs[b] < document).astype(jnp.int32) for b in range(BLOCKS)]))
    lane = lax.broadcasted_iota(jnp.int32, (1, ROWS), 1)
    start_row = jnp.where(lane < BLK, starts[0], starts[1])

    dqt[...] = jnp.zeros_like(dqt)
    for load in q_loads + g_loads:
        load.wait()

    key_at = lax.broadcasted_iota(jnp.int32, (ROWS, ROWS), 0)
    query_at = lax.broadcasted_iota(jnp.int32, (ROWS, ROWS), 1)
    far = 2 * FAR

    def shifted_exp(s, row, bias):
        return jnp.concatenate(
            [jnp.exp2(s[b * BLK:(b + 1) * BLK] * LOG2_SCALE - (row - bias[b])) for b in range(2)], axis=0
        )

    def tile_stats(d, first):
        key_block = 2 * (c - d)
        bias = [jnp.where(key_block + b >= start_row, 0.0, NEGATIVE) for b in range(2)]
        for h in range(GROUP):
            s = dot_nt(kv[d, 0], qs[h])
            gp = dot_nt(kv[d, 1], gs[h])
            gps[d, h] = gp
            if first:
                s = jnp.where(key_at <= query_at, s, NEGATIVE)
            new = jnp.maximum(*[
                jnp.max(s[b * BLK:(b + 1) * BLK], axis=0, keepdims=True) * LOG2_SCALE + bias[b] for b in range(2)
            ])
            if not first:
                old = top[h]
                new = jnp.maximum(old, new)
            halves = [jnp.exp2(s[b * BLK:(b + 1) * BLK] * LOG2_SCALE - (new - bias[b])) for b in range(2)]
            part = jnp.sum(halves[0] + halves[1], axis=0, keepdims=True)
            part_weighted = jnp.sum(halves[0] * gp[:BLK] + halves[1] * gp[BLK:], axis=0, keepdims=True)
            if not first:
                factor = jnp.exp2(old - new)
                part = total[h] * factor + part
                part_weighted = weighted[h] * factor + part_weighted
            top[h] = new
            tops[d, h] = new
            total[h] = part
            weighted[h] = part_weighted
            for b in range(2):
                ws[h, d, b * BLK:(b + 1) * BLK] = halves[b].astype(BF16)

    def far_stats():
        bias = jnp.where(2 * (c - far) + 1 >= starts[0], 0.0, NEGATIVE)
        for h in range(GROUP):
            s = dot_nt(kv[far, 0, BLK:], qs[h, :BLK])
            gp = dot_nt(kv[far, 1, BLK:], gs[h, :BLK])
            old = top[h, :, :BLK]
            new = jnp.maximum(old, jnp.max(s, axis=0, keepdims=True) * LOG2_SCALE + bias)
            w = jnp.exp2(s * LOG2_SCALE - (new - bias))
            factor = jnp.exp2(old - new)
            top[h, :, :BLK] = new
            tops[far, h, :, :BLK] = new
            total[h, :, :BLK] = total[h, :, :BLK] * factor + jnp.sum(w, axis=0, keepdims=True)
            weighted[h, :, :BLK] = weighted[h, :, :BLK] * factor + jnp.sum(w * gp, axis=0, keepdims=True)
            far_ws[h] = w.astype(BF16)
            far_gps[h] = gp

    tile_stats(0, True)

    for i in range(RING - 1):
        for load in loads(i):
            load.start()
    kt[:, :ROWS] = jnp.transpose(kv[0, 0].astype(F32)).astype(BF16)

    def near(d, carry):
        m = (d + 1) // 2

        @pl.when((d % 2 == 1) & (chip >= m))
        def _():
            key_copy(m).wait_recv()

            @pl.when(passes(m))
            def _():
                pass_copy(m).start()

        @pl.when(c >= d)
        def _():
            @pl.when(d % 2 == 1)
            def _():
                remote(kv.at[d], kv.at[d], pass_send.at[0], kv_recv.at[d], ctx=sibling).wait_recv()

            tile_stats(d, False)
            kt[:, pl.ds(pl.multiple_of(d * ROWS, ROWS), ROWS)] = jnp.transpose(kv[d, 0].astype(F32)).astype(BF16)

        @pl.when(c < d)
        def _():
            kt[:, pl.ds(pl.multiple_of(d * ROWS, ROWS), ROWS)] = jnp.zeros((HEAD_DIM, ROWS), BF16)
            for h in range(GROUP):
                ws[h, d] = jnp.zeros((ROWS, ROWS), BF16)

        return carry

    lax.fori_loop(1, far, near, 0)

    @pl.when(c >= far)
    def _():
        far_stats()

    for h in range(GROUP):
        inverse = 1.0 / total[h]
        total[h] = inverse
        weighted[h] = weighted[h] * inverse

    def tile_grads(d):
        sides = []
        for h in range(GROUP):
            p = ws[h, d].astype(F32) * (jnp.exp2(tops[d, h] - top[h]) * total[h])
            ds = (p * (gps[d, h] - weighted[h])).astype(BF16)
            sides.append((ds, p.astype(BF16)))
            if h % 2 == 1:
                both = pl.ds(h - 1, 2)
                key_part = dot_nn(jnp.concatenate([one[0] for one in sides], axis=1), qs[both].reshape(2 * ROWS, HEAD_DIM))
                value_part = dot_nn(jnp.concatenate([one[1] for one in sides], axis=1), gs[both].reshape(2 * ROWS, HEAD_DIM))
                sides = []
                if h == 1:
                    acc[0] = key_part
                    acc[1] = value_part
                else:
                    acc[0] += key_part
                    acc[1] += value_part
            ws[h, d] = ds

    def far_grads():
        far_kt[...] = jnp.transpose(kv[far, 0, BLK:].astype(F32)).astype(BF16)
        acc[...] = jnp.zeros_like(acc)
        for h in range(GROUP):
            p = far_ws[h].astype(F32) * (jnp.exp2(tops[far, h, :, :BLK] - top[h, :, :BLK]) * total[h, :, :BLK])
            ds = (p * (far_gps[h] - weighted[h, :, :BLK])).astype(BF16)
            acc[0, BLK:] += dot_nn(ds, qs[h, :BLK])
            acc[1, BLK:] += dot_nn(p.astype(BF16), gs[h, :BLK])
            dqt[h, :, :BLK] = dot_nn(far_kt[...], ds)

    def pair_copy(d):
        slot = (d + 1 - 2 * core) // 2
        return remote(stage.at[d], pair.at[slot], pair_send.at[d // 2], pair_recv.at[slot], ctx=sibling)

    def pair_wait(m):
        remote(stage.at[0], pair.at[m], pair_send.at[0], pair_recv.at[m], ctx=sibling).wait_recv()

    def back_copy(m):
        return remote(stage.at[2 * m], back.at[m], back_send.at[m], back_recv.at[m], ctx=(c + size - 2 * m) % size)

    def inward(step, carry):
        m = FAR - step // 2
        d = 2 * m - 1 + step % 2

        @pl.when((d < far) & (c >= d))
        def _():
            tile_grads(d)

        @pl.when((d == far) & (c >= d))
        def _():
            far_grads()

        @pl.when((step % 2 == 0) & (c >= d))
        def _():
            stage[d] = acc[...].astype(BF16)
            pair_copy(d).start()

        @pl.when((step % 2 == 1) & (c >= d))
        def _():
            @pl.when((m < FAR) | (core == 1))
            def _():
                pair_wait(m)
                acc[...] += pair[m].astype(F32)

            stage[d] = acc[...].astype(BF16)
            back_copy(m).start()

        return carry

    lax.fori_loop(0, far, inward, 0)
    tile_grads(0)

    places = (c * ROWS + lax.broadcasted_iota(jnp.int32, (ROWS, HEAD_DIM), 0)).astype(F32)
    lanes = lax.broadcasted_iota(jnp.int32, (ROWS, HEAD_DIM), 1)
    half = HEAD_DIM // 2
    pair_lane = jnp.where(lanes < half, lanes, lanes - half).astype(F32)
    angles = places * jnp.exp(pair_lane * (-2.0 * math.log(THETA) / HEAD_DIM))
    cosine[...] = jnp.cos(angles)
    sine[...] = jnp.where(lanes < half, 1.0, -1.0) * jnp.sin(angles)

    def rope_back(y):
        return y * cosine[...] + pltpu.roll(y, half, 1) * sine[...]

    for h in range(GROUP):
        gradient = dqt[h] + dot_nn(kt[...], ws[h].reshape(far * ROWS, ROWS))
        a_ref[:, h * HEAD_DIM:(h + 1) * HEAD_DIM] = rope_back(jnp.transpose(gradient) * SCALE).astype(BF16)

    for i in range(EARLY):
        for load in loads(i):
            load.wait()
        for kind in range(2):
            early[2 * i + kind] = dot_nt(a_ref[:, :base], w[i, kind * WIDE:(kind + 1) * WIDE, :base])

    @pl.when(core == 0)
    def _():
        pair_wait(0)
        acc[...] += pair[0].astype(F32)

    for m in range(FAR, 0, -1):
        @pl.when(chip + m < chips)
        def _():
            back_copy(m).wait_recv()
            acc[...] += back[m].astype(F32)

    a_ref[:, base:base + HEAD_DIM] = rope_back(acc[0] * SCALE).astype(BF16)
    a_ref[:, base + HEAD_DIM:DEPTH] = acc[1].astype(BF16)

    kept_half = (((z + 1) // 2) % 2, z // 2)
    kept_part = (z // 2, z % 2)

    def order(i, kind):
        x_first = i == X_STEP
        half = kept_half[kind]
        return (
            jnp.where(x_first, x, half),
            jnp.where(x_first, half, x),
            jnp.where(x_first, across, z_pairs[kind]),
            jnp.where(x_first, z_pairs[kind], across),
        )

    def first_copy(i, kind):
        n = 2 * i + kind
        kept, _, partner, _ = order(i, kind)
        return remote(s1.at[n, 1 - kept], r1.at[n], s1_send.at[n], s1_recv.at[n], tp=partner)

    def second_copy(i, kind):
        n = 2 * i + kind
        _, kept, _, partner = order(i, kind)
        return remote(s2.at[n, 1 - kept], r2.at[n], s2_send.at[n], s2_recv.at[n], tp=partner)

    def third_copy(i, kind):
        n = 2 * i + kind
        return remote(s3.at[n, 1 - kept_part[kind]], r3.at[n], s3_send.at[n], s3_recv.at[n], tp=z_pairs[1 - kind])

    def compute(i):
        @pl.when(i + RING - 1 < STEPS)
        def _():
            for load in loads(i + RING - 1):
                load.start()

        @pl.when(i >= EARLY)
        def _():
            for load in loads(i):
                load.wait()

        for kind in range(2):
            n = 2 * i + kind
            place = 2 * jnp.minimum(i, EARLY - 1) + kind

            @pl.when(i < EARLY)
            def _():
                early[place] += dot_nt(a_ref[:, base:], w[i % RING, kind * WIDE:(kind + 1) * WIDE, base:])

            @pl.when(i >= EARLY)
            def _():
                early[place] = dot_nt(a_ref[...], w[i % RING, kind * WIDE:(kind + 1) * WIDE, :])

            product = early[place].astype(BF16)
            for to_z in range(4):
                half = ((to_z + 1) // 2 % 2, to_z // 2)[kind]
                part = (to_z // 2, to_z % 2)[kind]
                for to_x in range(2):
                    rows = to_z * 64 + to_x * 32
                    outer = jnp.where(i == X_STEP, to_x, half)
                    inner = jnp.where(i == X_STEP, half, to_x)
                    to = pl.multiple_of(inner * 64 + part * 32, 32)
                    s1[n, outer, pl.ds(to, 32)] = product[rows:rows + 32]
            first_copy(i, kind).start()

    def second(i):
        for kind in range(2):
            n = 2 * i + kind
            first_copy(i, kind).wait_recv()
            value = (s1[n, order(i, kind)[0]].astype(F32) + r1[n].astype(F32)).astype(BF16)
            s2[n, 0] = value[:64]
            s2[n, 1] = value[64:]
            second_copy(i, kind).start()

    def third(i):
        for kind in range(2):
            n = 2 * i + kind
            second_copy(i, kind).wait_recv()
            value = (s2[n, order(i, kind)[1]].astype(F32) + r2[n].astype(F32)).astype(BF16)
            s3[n, 0] = value[:32]
            s3[n, 1] = value[32:]
            third_copy(i, kind).start()

    def last(i):
        for kind in range(2):
            n = 2 * i + kind
            third_copy(i, kind).wait_recv()
            value = s3[n, kept_part[kind]].astype(F32) + r3[n].astype(F32)
            out_ref[:, pl.ds(i * WIDTH + kind * WIDE, WIDE)] = value.astype(BF16)

    def step(i, carry):
        @pl.when(i < STEPS)
        def _():
            compute(i)

        for number, work in enumerate((second, third, last)):
            lag = (number + 1) * LAG

            @pl.when((i >= lag) & (i < STEPS + lag))
            def _():
                work(i - lag)

        return carry

    lax.fori_loop(0, STEPS + 3 * LAG, step, 0)

    def drain(i, carry):
        for kind in range(2):
            first_copy(i, kind).wait_send()
            second_copy(i, kind).wait_send()
            third_copy(i, kind).wait_send()
        return carry

    lax.fori_loop(0, STEPS, drain, 0)

    for m in range(FAR + 1):
        @pl.when(passes(m))
        def _():
            pass_copy(m).wait_send()

    for m in range(1, FAR + 1):
        @pl.when(chip + m < chips)
        def _():
            key_copy(m).wait_send()

        @pl.when(c >= 2 * m - 1)
        def _():
            pair_copy(2 * m - 1).wait_send()

        @pl.when(chip >= m)
        def _():
            back_copy(m).wait_send()


def layer(q, k, v, g, docs, wq, wk, wv):
    any_spec = pl.BlockSpec(memory_space=pl.ANY)
    slots = 2 * FAR + 1
    dma = pltpu.SemaphoreType.DMA
    width = wq.shape[0]
    chunks = 2 * STEPS
    return pl.pallas_call(
        layer_kernel,
        out_shape=pltpu.VMEM((ROWS // 8, width), BF16),
        in_specs=[any_spec] * 4 + [pl.BlockSpec(memory_space=pltpu.SMEM)] + [any_spec] * 3,
        out_specs=pl.BlockSpec(memory_space=pltpu.VMEM),
        scratch_shapes=[
            pltpu.VMEM((slots, 2, ROWS, HEAD_DIM), BF16),
            pltpu.VMEM((GROUP, ROWS, HEAD_DIM), BF16),
            pltpu.VMEM((GROUP, ROWS, HEAD_DIM), BF16),
            pltpu.VMEM((GROUP, slots - 1, ROWS, ROWS), BF16),
            pltpu.VMEM((slots - 1, GROUP, ROWS, ROWS), F32),
            pltpu.VMEM((GROUP, BLK, BLK), BF16),
            pltpu.VMEM((GROUP, BLK, BLK), F32),
            pltpu.VMEM((slots, GROUP, 1, ROWS), F32),
            pltpu.VMEM((GROUP, 1, ROWS), F32),
            pltpu.VMEM((GROUP, 1, ROWS), F32),
            pltpu.VMEM((GROUP, 1, ROWS), F32),
            pltpu.VMEM((GROUP, HEAD_DIM, ROWS), F32),
            pltpu.VMEM((HEAD_DIM, (slots - 1) * ROWS), BF16),
            pltpu.VMEM((HEAD_DIM, BLK), BF16),
            pltpu.VMEM((2, ROWS, HEAD_DIM), F32),
            pltpu.VMEM((slots, 2, ROWS, HEAD_DIM), BF16),
            pltpu.VMEM((FAR + 1, 2, ROWS, HEAD_DIM), BF16),
            pltpu.VMEM((FAR + 1, 2, ROWS, HEAD_DIM), BF16),
            pltpu.VMEM((ROWS, HEAD_DIM), F32),
            pltpu.VMEM((ROWS, HEAD_DIM), F32),
            pltpu.VMEM((ROWS, DEPTH), BF16),
            pltpu.VMEM((2 * EARLY, ROWS, WIDE), F32),
            pltpu.VMEM((RING, WIDTH, DEPTH), BF16),
            pltpu.VMEM((chunks, 2, 128, WIDE), BF16),
            pltpu.VMEM((chunks, 128, WIDE), BF16),
            pltpu.VMEM((chunks, 2, 64, WIDE), BF16),
            pltpu.VMEM((chunks, 64, WIDE), BF16),
            pltpu.VMEM((chunks, 2, 32, WIDE), BF16),
            pltpu.VMEM((chunks, 32, WIDE), BF16),
            dma((GROUP,)),
            dma((GROUP,)),
            dma((2,)),
            dma((FAR + 1,)),
            dma((slots,)),
            dma((FAR + 1,)),
            dma((FAR + 1,)),
            dma((FAR + 1,)),
            dma((FAR + 1,)),
            dma((FAR + 1,)),
            dma((RING, 3)),
        ] + [dma((chunks,))] * 6,
        compiler_params=pltpu.CompilerParams(
            collective_id=0, has_side_effects=True, vmem_limit_bytes=60 * 1024 * 1024
        ),
        name="layer",
    )(q, k, v, g, docs, wq, wk, wv)


def local(query_rows, key_rows, value_rows, grad_out, doc_ids, w_query, w_key, w_value):
    return layer(query_rows, key_rows, value_rows, grad_out, doc_ids, w_query, w_key, w_value)


def solution(mesh):
    in_specs = (
        P("ctx", "tp"),
        P("ctx", "tp"),
        P("ctx", "tp"),
        P("ctx", "tp"),
        P(),
        P(None, "tp"),
        P(None, "tp"),
        P(None, "tp"),
    )
    out_specs = P(("ctx", "tp"), None)
    return jax.shard_map(local, mesh=mesh, in_specs=in_specs, out_specs=out_specs, check_vma=False)
```
